256 devices in a mesh: dp: 64 (over y, x, z_lo), ulysses: 4 (over z_hi, core).
Axes of the slice: x: 4, y: 4, z: 8 (z_hi: 2, z_lo: 4; z = z_hi * 4 + z_lo), core: 2. Of those that a mesh axis runs over, the one named last changes fastest.
Arguments:
- queries: bfloat16 [65536, 2560], P(('dp', 'ulysses')), may hold values from -6 to 6
- key_rows: bfloat16 [65536, 2560], P(('dp', 'ulysses')), may hold values from -6 to 6
- values: bfloat16 [65536, 2560], P(('dp', 'ulysses')), may hold values from -6 to 6
- out_grad: bfloat16 [65536, 2560], P(('dp', 'ulysses')), may hold values from -16 to 16
- frames: int32 [64, 2], replicated, may hold values from 1 to 8, as said below
- offsets: int32 [64, 2], replicated, may hold values from 0 to 960, as said below
Outputs:
- attended: bfloat16 [65536, 2560], P(('dp', 'ulysses'))
- query_grad: bfloat16 [65536, 2560], P(('dp', 'ulysses'))
- key_grad: bfloat16 [65536, 2560], P(('dp', 'ulysses'))
- value_grad: bfloat16 [65536, 2560], P(('dp', 'ulysses'))
The draws below stay inside these ranges and needn't reach their ends.
Inputs may be any that keep to these rules, and one draw needn't show every extreme that they name: Some group holds two clips of 8 frames in every draw. `offsets`: each a multiple of 64; a group's clips lie in order, apart, inside its 1024 rows.
All inputs are finite; a program needn't handle non-finite values.
Results may differ from the reference program's by a relative error of at most 0.012.
Values may be sent and summed in bfloat16 or wider, within the bound.
No kernel may reach another device: no remote copies, remote signals or barrier semaphores. Data moves between devices by JAX's collectives and lax.ppermute only.
A program may use at most 128 MiB of HBM per device.

```python
import math
import jax
import jax.numpy as jnp
from jax import lax

HEADS = 20
HD = 128
FPT = 64
FRAMES_G = 16
NCLIP = 2
CLIP_FRAMES = 8
CLIP_ROWS = 512
TOKENS = 65536
N_DP = 64


def clip_plan(key):
    frame_key = jax.random.fold_in(key, 0)
    chosen_key = jax.random.fold_in(key, 1)
    first_key = jax.random.fold_in(key, 2)
    second_key = jax.random.fold_in(key, 3)
    short_key = jax.random.fold_in(key, 5)
    frames = jax.random.randint(frame_key, (N_DP, NCLIP), 1, CLIP_FRAMES + 1)
    full_group = jax.random.randint(chosen_key, (), 0, N_DP)
    short_group = (full_group + 1 + jax.random.randint(short_key, (), 0, N_DP - 1)) % N_DP
    chosen = (jnp.arange(N_DP) == full_group)[:, None]
    is_short = jnp.arange(N_DP) == short_group
    frames = jnp.where(chosen, CLIP_FRAMES, frames)
    frames = jnp.where(is_short[:, None] & (jnp.arange(NCLIP) == 1)[None, :], 1, frames).astype(jnp.int32)
    slack = FRAMES_G - jnp.sum(frames, axis=1)
    first_gap = jax.random.randint(first_key, (N_DP,), 0, slack + 1)
    second_gap = jax.random.randint(second_key, (N_DP,), 0, slack - first_gap + 1)
    second_gap = jnp.where(is_short, slack - first_gap, second_gap)
    starts = (jnp.stack([first_gap, first_gap + frames[:, 0] + second_gap], axis=1) * FPT).astype(jnp.int32)
    return (frames, starts)


def draw_frames(key, part):
    frames, starts = clip_plan(key)
    return frames


def draw_offsets(key, part):
    frames, starts = clip_plan(key)
    return starts


def draw_queries(key, part):
    key = jax.random.fold_in(key, 3)
    drawn = jnp.clip(jax.random.normal(key, (TOKENS, HEADS * HD), jnp.float32), -6.0, 6.0)
    return drawn.astype(jnp.bfloat16)


def draw_key_rows(key, part):
    key = jax.random.fold_in(key, 7)
    drawn = jnp.clip(jax.random.normal(key, (TOKENS, HEADS * HD), jnp.float32), -6.0, 6.0)
    return drawn.astype(jnp.bfloat16)


def level_of(rng, extent, cuts, least, top_value):
    level = 1.0
    for dim, parts in cuts:
        heights = jax.random.uniform(jax.random.fold_in(jax.random.fold_in(rng, 6), dim), (parts,), jnp.float32, least / len(cuts), top_value / len(cuts))
        level = level * jnp.repeat(jnp.exp(heights), extent[dim] // parts).reshape((-1,) + (1,) * (len(extent) - 1 - dim))
    return level


def noise(own_key, extent, deviation, bound, shards=(), held_as=jnp.bfloat16):
    gain = level_of(own_key, extent, shards, -0.22, 0.18) if shards else 1.0
    entries = jax.random.normal(own_key, extent, jnp.float32) * deviation * gain
    return jnp.minimum(jnp.maximum(entries, -bound), bound).astype(held_as)


def setup_inputs(seed: int = 0) -> dict:
    arg_keys = jax.random.split(jax.random.key(seed), 7)
    queries = draw_queries(jax.random.fold_in(arg_keys[6], 71), 0)
    key_rows = draw_key_rows(jax.random.fold_in(arg_keys[6], 71), 0)
    values = noise(arg_keys[2], (TOKENS, HEADS * HD), 1.0, 6.0, ((0, 256),))
    out_grad = noise(arg_keys[3], (TOKENS, HEADS * HD), 4.0, 16.0, ((0, 256),))
    frames = draw_frames(jax.random.fold_in(arg_keys[6], 71), 0)
    offsets = draw_offsets(jax.random.fold_in(arg_keys[6], 71), 0)
    return dict(queries=queries, key_rows=key_rows, values=values, out_grad=out_grad, frames=frames, offsets=offsets)


NEG_FILL = -1e+30

def attend_clip(queries, key_rows, values, out_grad, labels, head_count):
    row_count = queries.shape[0]
    head_width = queries.shape[1] // head_count
    score_scale = 1.0 / math.sqrt(head_width)
    q_heads = queries.reshape(row_count, head_count, head_width).astype(jnp.float32)
    k_heads = key_rows.reshape(row_count, head_count, head_width).astype(jnp.float32)
    v_heads = values.reshape(row_count, head_count, head_width).astype(jnp.float32)
    g_heads = out_grad.reshape(row_count, head_count, head_width).astype(jnp.float32)
    row_valid = labels >= 0
    same_clip = (labels[:, None] == labels[None, :]) & row_valid[:, None]
    scores = jnp.einsum('qhd,khd->hqk', q_heads, k_heads) * score_scale
    masked = jnp.where(same_clip[None], scores, NEG_FILL)
    row_max = jnp.where(row_valid[None, :], lax.optimization_barrier(jnp.max(masked, axis=2)), 0.0)
    exp_scores = jnp.where(same_clip[None], jnp.exp(masked - row_max[:, :, None]), 0.0)
    row_total = jnp.where(row_valid[None, :], lax.optimization_barrier(jnp.sum(exp_scores, axis=2)), 1.0)
    probs = exp_scores / row_total[:, :, None]
    probs_low = probs.astype(jnp.bfloat16).astype(jnp.float32)
    attended_full = jnp.einsum('hqk,khd->qhd', probs_low, v_heads)
    dot_term = lax.optimization_barrier(jnp.sum(g_heads * attended_full, axis=2)).T
    dprobs = jnp.einsum('qhd,khd->hqk', g_heads, v_heads)
    dscore = (score_scale * probs * (dprobs - dot_term[:, :, None])).astype(jnp.bfloat16).astype(jnp.float32)
    query_grad = jnp.einsum('hqk,khd->qhd', dscore, k_heads)
    key_grad = jnp.einsum('hqk,qhd->khd', dscore, q_heads)
    value_grad = jnp.einsum('hqk,qhd->khd', probs_low, g_heads)
    shape_out = (row_count, head_count * head_width)
    return (attended_full.reshape(shape_out).astype(jnp.bfloat16), query_grad.reshape(shape_out).astype(jnp.bfloat16), key_grad.reshape(shape_out).astype(jnp.bfloat16), value_grad.reshape(shape_out).astype(jnp.bfloat16))

def reference(queries, key_rows, values, out_grad, frames, offsets):
    feature_count = queries.shape[1]
    group_rows = FRAMES_G * FPT

    def one_group(group_index):
        row_start = (group_index * group_rows).astype(jnp.int32)
        pieces = [lax.dynamic_slice_in_dim(array, row_start, group_rows, 0) for array in (queries, key_rows, values, out_grad)]
        padded = [jnp.concatenate([piece, jnp.zeros((CLIP_ROWS, feature_count), piece.dtype)], axis=0) for piece in pieces]
        totals = [jnp.zeros((group_rows + CLIP_ROWS, feature_count), jnp.float32) for piece in pieces]
        for clip_index in range(NCLIP):
            clip_begin = offsets[group_index, clip_index].astype(jnp.int32)
            clip_length = frames[group_index, clip_index] * FPT
            sliced = [lax.dynamic_slice_in_dim(array, clip_begin, CLIP_ROWS, 0) for array in padded]
            labels = jnp.where(jnp.arange(CLIP_ROWS, dtype=jnp.int32) < clip_length, 0, -1).astype(jnp.int32)
            results = attend_clip(sliced[0], sliced[1], sliced[2], sliced[3], labels, HEADS)
            totals = [total + lax.dynamic_update_slice_in_dim(jnp.zeros_like(total), result.astype(jnp.float32), clip_begin, 0) for total, result in zip(totals, results)]
        return tuple((total[:group_rows].astype(jnp.bfloat16) for total in totals))
    outputs = lax.map(one_group, jnp.arange(N_DP, dtype=jnp.int32))
    shape_out = (N_DP * group_rows, feature_count)
    return (outputs[0].reshape(shape_out), outputs[1].reshape(shape_out), outputs[2].reshape(shape_out), outputs[3].reshape(shape_out))
```

```python
import math

import jax
import jax.numpy as jnp
from jax import lax
from jax.experimental import pallas as pl
from jax.experimental.pallas import tpu as pltpu
from jax.sharding import PartitionSpec as P

HEADS = 20
HD = 128
FPT = 64
FPT_BITS = 6
HALF = 512
OWN = 256
MINE = 10
COLS = MINE * HD
NEG_FILL = -1e30
SCALE = 1.0 / math.sqrt(HD)
LOG2E = math.log2(math.e)
ROWS_STEP = 256
JOIN_STEPS = 5

SLOTS = (0, 5, 8, 10, 12, 15, 18, 20)


CORE, B0, E0, B1, E1, PA, PB, FIRST, COUNT, NEAR, FAR, NEARROW, FARROW, AWAY, BRANCH = range(15)


def split_heads(a, b):
    best, heads = jnp.maximum(a, b * (MINE - 1)), 1
    for h in range(2, MINE):
        cost = jnp.maximum(a * h, b * (MINE - h))
        heads = jnp.where(cost < best, h, heads)
        best = jnp.minimum(cost, best)
    return heads, jnp.where((a > 0) & (b > 0), best, 0)


def fill_plan(plan, place, frames, offsets):
    group, core, high = place[0], place[1] & 1, place[1] >> 1
    base = high * HALF
    a = b = 0
    for i, (begin_at, end_at) in enumerate(((B0, E0), (B1, E1))):
        begin = offsets[group, i]
        end = begin + frames[group, i] * FPT
        crosses = (begin < HALF) & (end > HALF)
        a = jnp.where(crosses, (HALF - begin) >> FPT_BITS, a)
        b = jnp.where(crosses, (end - HALF) >> FPT_BITS, b)
        plan[begin_at] = jnp.where(crosses, 0, begin - base)
        plan[end_at] = jnp.where(crosses, 0, end - base)
    h, cost = split_heads(a, b)
    branch = 0
    for i, n in enumerate(SLOTS[:-1]):
        branch = jnp.where(cost > n, i + 1, branch)
    second = high == 1
    plan[CORE] = core
    plan[PA] = FPT * a
    plan[PB] = FPT * b
    plan[FIRST] = jnp.where(second, 0, h)
    plan[COUNT] = jnp.where(second, h, MINE - h)
    plan[NEAR] = jnp.where(second, b, a)
    plan[FAR] = jnp.where(second, a, b)
    plan[NEARROW] = jnp.where(second, 0, HALF - FPT * a)
    plan[FARROW] = jnp.where(second, HALF - FPT * a, 0)
    plan[AWAY] = jnp.where(second, h, 0)
    plan[BRANCH] = branch


def local_row(plan, position):
    return (position + OWN * plan[CORE]) & (HALF - 1)


def near_clips(plan, position):
    row = local_row(plan, position)
    first = (row >= plan[B0]) & (row < plan[E0])
    second = (row >= plan[B1]) & (row < plan[E1])
    return jnp.where(first, 0, jnp.where(second, 1, -1))


def cross_clip(plan, position):
    row = local_row(plan, position)
    return jnp.where((row < plan[PB]) | (row >= HALF - plan[PA]), 0, -1)


def dot(x, y, dims):
    return lax.dot_general(x, y, (dims, ((), ())), preferred_element_type=jnp.float32)


def attend(label_of, rows, results):
    columns = label_of(lax.broadcasted_iota(jnp.int32, (1, HALF), 1))
    k, v = rows[1], rows[2]
    blocks = [pl.ds(start, ROWS_STEP) for start in range(0, HALF, ROWS_STEP)]
    labels = [
        label_of(block.start + lax.broadcasted_iota(jnp.int32, (ROWS_STEP, 1), 0))
        for block in blocks
    ]
    q = [rows[0, block, :] for block in blocks]
    g = [rows[3, block, :].astype(jnp.float32) for block in blocks]
    scores = [dot(x, k, ((1,), (1,))) for x in q]
    masked = [jnp.where(x == columns, s, NEG_FILL) for x, s in zip(labels, scores)]
    row_max = [jnp.max(s, axis=1, keepdims=True) for s in masked]
    e = [jnp.exp2((s - m) * (SCALE * LOG2E)) for s, m in zip(masked, row_max)]
    row_total = [jnp.sum(x, axis=1, keepdims=True) for x in e]
    inverse = [jnp.where(x >= 0, 1.0 / t, 0.0) for x, t in zip(labels, row_total)]
    e_low = [x.astype(jnp.bfloat16) for x in e]
    attended = [dot(x, v, ((1,), (0,))) * i for x, i in zip(e_low, inverse)]
    g_low = [(x * i).astype(jnp.bfloat16) for x, i in zip(g, inverse)]
    dprobs = [dot(x, v, ((1,), (1,))) for x in g_low]
    dot_term = [
        jnp.sum(x.astype(jnp.float32) * y, axis=1, keepdims=True) for x, y in zip(g_low, attended)
    ]
    dscore = [(x * (d - t)).astype(jnp.bfloat16) for x, d, t in zip(e, dprobs, dot_term)]
    query_grad = [dot(x, k, ((1,), (0,))) * SCALE for x in dscore]
    for block, x, y in zip(blocks, attended, query_grad):
        results[0, block, :] = x.astype(jnp.bfloat16)
        results[1, block, :] = y.astype(jnp.bfloat16)
    key_grad = sum(dot(x, y, ((0,), (0,))) for x, y in zip(q, dscore))
    value_grad = sum(dot(x, y, ((0,), (0,))) for x, y in zip(g_low, e_low))
    results[2] = (key_grad.T * SCALE).astype(jnp.bfloat16)
    results[3] = value_grad.T.astype(jnp.bfloat16)


def gather_rows(q, k, v, g, peer, rows):
    for i, mine in enumerate((q, k, v, g)):
        rows[i, :OWN, :] = mine[...]
    rows[:, OWN:, :] = peer[...]


def near_kernel(plan, q, k, v, g, peer, out_0, out_1, out_2, out_3, peer_out, rows, results):
    gather_rows(q, k, v, g, peer, rows)
    attend(lambda position: near_clips(plan, position), rows, results)
    for i, out in enumerate((out_0, out_1, out_2, out_3)):
        out[...] = results[i, :OWN, :]
    peer_out[...] = results[:, OWN:, :]


def cross_kernel(plan, q, k, v, g, peer, arrived, *rest):
    before, after, (leaving, rows, results) = rest[:5], rest[5:10], rest[10:]
    step = pl.program_id(0)
    far = plan[FAR]

    def place(frame):
        return pl.ds(pl.multiple_of(local_row(plan, plan[FARROW] + FPT * frame), FPT), FPT)

    def take(frame, carry):
        rows[:, place(frame), :] = arrived[step * far + frame]
        return carry

    def give(frame, carry):
        leaving[step * far + frame] = results[:, place(frame), :]
        return carry

    def near_rows(start):
        row = local_row(plan, start + lax.broadcasted_iota(jnp.int32, (OWN, HD), 0))
        return (row >= plan[NEARROW]) & (row < plan[NEARROW] + FPT * plan[NEAR])

    @pl.when(step < plan[COUNT])
    def _():
        gather_rows(q, k, v, g, peer, rows)
        lax.fori_loop(0, far, take, 0)
        attend(lambda position: cross_clip(plan, position), rows, results)
        lax.fori_loop(0, far, give, 0)
        own_near, peer_near = near_rows(0), near_rows(OWN)
        for i in range(4):
            after[i][...] = jnp.where(own_near, results[i, :OWN, :], before[i][...])
            after[4][i] = jnp.where(peer_near, results[i, OWN:, :], before[4][i])


def head_specs(head):
    own = [pl.BlockSpec((OWN, HD), lambda i, plan: (0, plan[CORE] * MINE + head(i, plan)))] * 4
    half = pl.BlockSpec((4, OWN, HD), lambda i, plan: (0, 0, head(i, plan)))
    return own, half


HEAD_SCRATCH = [pltpu.VMEM((4, HALF, HD), jnp.bfloat16)] * 2
PARAMS = pltpu.CompilerParams(vmem_limit_bytes=40 * 1024 * 1024)
HALF_SHAPE = jax.ShapeDtypeStruct((4, OWN, COLS), jnp.bfloat16)
OUT_SHAPES = [jax.ShapeDtypeStruct((OWN, HEADS * HD), jnp.bfloat16)] * 4


def near_call(plan, arrays, peer):
    own, half = head_specs(lambda i, plan: i)
    return pl.pallas_call(
        near_kernel,
        grid_spec=pltpu.PrefetchScalarGridSpec(
            num_scalar_prefetch=1,
            grid=(MINE,),
            in_specs=own + [half],
            out_specs=own + [half],
            scratch_shapes=HEAD_SCRATCH,
        ),
        out_shape=OUT_SHAPES + [HALF_SHAPE],
        compiler_params=PARAMS,
        name="near_clips",
    )(plan, *arrays, peer)


def cross_call(plan, arrays, peer, arrived, results):
    own, half = head_specs(lambda i, plan: plan[FIRST] + jnp.minimum(i, plan[COUNT] - 1))
    whole = pl.BlockSpec(arrived.shape, lambda i, plan: (0, 0, 0, 0))
    return pl.pallas_call(
        cross_kernel,
        grid_spec=pltpu.PrefetchScalarGridSpec(
            num_scalar_prefetch=1,
            grid=(MINE,),
            in_specs=own + [half, whole] + own + [half],
            out_specs=own + [half, whole],
            scratch_shapes=HEAD_SCRATCH,
        ),
        out_shape=OUT_SHAPES + [HALF_SHAPE, jax.ShapeDtypeStruct(arrived.shape, jnp.bfloat16)],
        input_output_aliases={7 + i: i for i in range(5)},
        compiler_params=PARAMS,
        name="cross_clip",
    )(plan, *arrays, peer, arrived, *results)


ANY = pl.BlockSpec(memory_space=pl.ANY)


def near_slots(plan, body):
    near = plan[NEAR]

    def one_head(head, carry):
        def one(frame, carry):
            row = pl.multiple_of(plan[NEARROW] + FPT * frame, FPT)
            body(head * near + frame, plan[AWAY] + head, row)
            return carry

        return lax.fori_loop(0, near, one, carry)

    lax.fori_loop(0, MINE - plan[COUNT], one_head, 0)


SMEM = pl.BlockSpec(memory_space=pltpu.SMEM)
VMEM = pl.BlockSpec(memory_space=pltpu.VMEM)


def split_kernel(place, frames, offsets, q, k, v, g, plan, out, sems):
    col = pl.ds(pl.multiple_of((1 - (place[1] & 1)) * COLS, COLS), COLS)
    copies = [
        pltpu.make_async_copy(x.at[:, col], out.at[i], sems.at[i])
        for i, x in enumerate((q, k, v, g))
    ]
    for c in copies:
        c.start()
    fill_plan(plan, place, frames, offsets)
    for c in copies:
        c.wait()


def split_call(place, frames, offsets, arrays):
    return pl.pallas_call(
        split_kernel,
        in_specs=[SMEM] * 3 + [ANY] * 4,
        out_specs=[SMEM, VMEM],
        out_shape=[jax.ShapeDtypeStruct((BRANCH + 1,), jnp.int32), HALF_SHAPE],
        scratch_shapes=[pltpu.SemaphoreType.DMA((4,))],
        compiler_params=PARAMS,
        name="split_heads",
    )(place, frames, offsets, *arrays)


def pack_kernel(plan, q, k, v, g, peer, out, own_sem, peer_sem):
    def copies(slot, head, row, own):
        at = pl.ds(pl.multiple_of(row & (OWN - 1), FPT), FPT)
        if own:
            col = pl.ds(pl.multiple_of((plan[CORE] * MINE + head) * HD, HD), HD)
            return [
                pltpu.make_async_copy(x.at[at, col], out.at[slot, i], own_sem.at[slot, i])
                for i, x in enumerate((q, k, v, g))
            ]
        col = pl.ds(pl.multiple_of(head * HD, HD), HD)
        return [pltpu.make_async_copy(peer.at[:, at, col], out.at[slot], peer_sem.at[slot])]

    def each(act):
        def body(slot, head, row):
            mine = (row >= OWN) == (plan[CORE] == 1)

            @pl.when(mine)
            def _():
                for c in copies(slot, head, row, True):
                    act(c)

            @pl.when(jnp.logical_not(mine))
            def _():
                for c in copies(slot, head, row, False):
                    act(c)

        near_slots(plan, body)

    each(lambda c: c.start())
    each(lambda c: c.wait())


def pack_call(plan, arrays, peer):
    most = SLOTS[-1]
    return pl.pallas_call(
        pack_kernel,
        in_specs=[SMEM] + [ANY] * 5,
        out_specs=VMEM,
        out_shape=jax.ShapeDtypeStruct((most, 4, FPT, HD), jnp.bfloat16),
        scratch_shapes=[
            pltpu.SemaphoreType.DMA((most, 4)),
            pltpu.SemaphoreType.DMA((most,)),
        ],
        compiler_params=PARAMS,
        name="pack_cross",
    )(plan, *arrays, peer)


def join_kernel(plan, other, *rest):
    for i, out in enumerate(rest[4:]):
        out[...] = other[i]


def join_call(plan, other, outs):
    width = COLS // JOIN_STEPS
    block = pl.BlockSpec((OWN, width), lambda i, plan: (0, (1 - plan[CORE]) * JOIN_STEPS + i))
    return pl.pallas_call(
        join_kernel,
        grid_spec=pltpu.PrefetchScalarGridSpec(
            num_scalar_prefetch=1,
            grid=(JOIN_STEPS,),
            in_specs=[pl.BlockSpec((4, OWN, width), lambda i, plan: (0, 0, i))] + [ANY] * 4,
            out_specs=[block] * 4,
        ),
        out_shape=OUT_SHAPES,
        input_output_aliases={2 + i: i for i in range(4)},
        compiler_params=PARAMS,
        name="join_halves",
    )(plan, other, *outs)


def unpack_kernel(plan, mine, other, *rest):
    outs, sems = rest[4:8], rest[8]

    def each(act):
        def body(slot, head, row):
            @pl.when((row >= OWN) == (plan[CORE] == 1))
            def _():
                at = pl.ds(pl.multiple_of(row & (OWN - 1), FPT), FPT)
                for j, back in enumerate((mine, other)):
                    core = plan[CORE] if j == 0 else 1 - plan[CORE]
                    col = pl.ds(pl.multiple_of((core * MINE + head) * HD, HD), HD)
                    for i, out in enumerate(outs):
                        act(
                            pltpu.make_async_copy(
                                back.at[slot, i], out.at[at, col], sems.at[slot, j, i]
                            )
                        )

        near_slots(plan, body)

    each(lambda c: c.start())
    each(lambda c: c.wait())


def unpack_call(plan, mine, other, outs):
    return pl.pallas_call(
        unpack_kernel,
        in_specs=[SMEM, VMEM, VMEM] + [ANY] * 4,
        out_specs=[ANY] * 4,
        out_shape=OUT_SHAPES,
        input_output_aliases={3: 0, 4: 1, 5: 2, 6: 3},
        scratch_shapes=[pltpu.SemaphoreType.DMA((mine.shape[0], 2, 4))],
        compiler_params=PARAMS,
        name="unpack_cross",
    )(plan, mine, other, *outs)


OTHER_CORE = [(i, i ^ 1) for i in range(4)]
OTHER_CHIP = [(i, i ^ 2) for i in range(4)]


def make_branch(slots):
    def run(plan, arrays, peer, packed):
        if slots:
            arrived = lax.ppermute(packed[:slots], "ulysses", OTHER_CHIP)
        results = near_call(plan, arrays, peer)
        if slots:
            *results, leaving = cross_call(plan, arrays, peer, arrived, results)
            returned = lax.ppermute(leaving, "ulysses", OTHER_CHIP)
        other = lax.ppermute(results[4], "ulysses", OTHER_CORE)
        outs = join_call(plan, other, results[:4])
        if slots:
            returned_other = lax.ppermute(returned, "ulysses", OTHER_CORE)
            outs = unpack_call(plan, returned, returned_other, outs)
        return tuple(outs)

    return run


def shards(queries, key_rows, values, out_grad, frames, offsets):
    place = jnp.stack([lax.axis_index("dp"), lax.axis_index("ulysses")]).astype(jnp.int32)
    arrays = (queries, key_rows, values, out_grad)
    plan, sent = split_call(place, frames, offsets, arrays)
    peer = lax.ppermute(sent, "ulysses", OTHER_CORE)
    packed = pack_call(plan, arrays, peer)
    branches = [make_branch(n) for n in SLOTS]
    return lax.switch(plan[BRANCH], branches, plan, arrays, peer, packed)


def solution(mesh):
    rows = P(("dp", "ulysses"), None)
    return jax.shard_map(
        shards,
        mesh=mesh,
        in_specs=(rows, rows, rows, rows, P(), P()),
        out_specs=(rows, rows, rows, rows),
        check_vma=False,
    )
```

```python
import functools
import math

import jax
import jax.numpy as jnp
from jax import lax
from jax.experimental import pallas as pl
from jax.experimental.pallas import tpu as pltpu
from jax.sharding import PartitionSpec as P

HEADS = 20
HD = 128
FPT = 64
FPT_BITS = 6
HALF = 512
OWN = 256
MINE = 10
COLS = MINE * HD
NEG_FILL = -1e30
SCALE = 1.0 / math.sqrt(HD)
LOG2E = math.log2(math.e)
ROWS_STEP = 256
JOIN_STEPS = 5
NEAR_HEADS = 2

SLOTS = (20, 18, 16, 15, 12, 10, 8, 0)


CORE, B0, E0, B1, E1, PA, PB, FIRST, COUNT, NEAR, FAR, NEARROW, FARROW, AWAY, GONE, PAIR, PAIRS, BRANCH = range(18)


def split_heads(a, b):
    best, heads = jnp.maximum(a, b * (MINE - 1)), 1
    for h in range(2, MINE):
        cost = jnp.maximum(a * h, b * (MINE - h))
        heads = jnp.where(cost < best, h, heads)
        best = jnp.minimum(cost, best)
    return heads, jnp.where((a > 0) & (b > 0), best, 0)


def fill_plan(plan, place, frames, offsets):
    group, core, high = place[0], place[1] & 1, place[1] >> 1
    base = high * HALF
    a = b = 0
    for i, (begin_at, end_at) in enumerate(((B0, E0), (B1, E1))):
        begin = offsets[i, group]
        end = begin + frames[i, group] * FPT
        crosses = (begin < HALF) & (end > HALF)
        a = jnp.where(crosses, (HALF - begin) >> FPT_BITS, a)
        b = jnp.where(crosses, (end - HALF) >> FPT_BITS, b)
        plan[begin_at] = jnp.where(crosses, 0, begin - base)
        plan[end_at] = jnp.where(crosses, 0, end - base)
    h, cost = split_heads(a, b)
    branch = 0
    for i, n in enumerate(SLOTS[1:]):
        branch = jnp.where(cost <= n, i + 1, branch)
    second = high == 1
    plan[CORE] = core
    plan[PA] = FPT * a
    plan[PB] = FPT * b
    plan[FIRST] = jnp.where(second, 0, h)
    plan[COUNT] = jnp.where(cost == 0, 0, jnp.where(second, h, MINE - h))
    plan[GONE] = jnp.where(cost == 0, 0, jnp.where(second, MINE - h, h))
    plan[NEAR] = jnp.where(second, b, a)
    plan[FAR] = jnp.where(second, a, b)
    plan[NEARROW] = jnp.where(second, 0, HALF - FPT * a)
    plan[FARROW] = jnp.where(second, HALF - FPT * a, 0)
    plan[PAIR] = jnp.where(second, 0, h >> 1)
    plan[PAIRS] = jnp.where(cost == 0, 0, jnp.where(second, (h + 1) >> 1, MINE // 2 - (h >> 1)))
    plan[AWAY] = jnp.where(second, h, 0)
    plan[BRANCH] = branch


def local_row(plan, position):
    return (position + OWN * plan[CORE]) & (HALF - 1)


def near_clips(plan, position):
    row = local_row(plan, position)
    first = (row >= plan[B0]) & (row < plan[E0])
    second = (row >= plan[B1]) & (row < plan[E1])
    return jnp.where(first, 0, jnp.where(second, 1, -1))


def cross_clip(plan, position):
    row = local_row(plan, position)
    return jnp.where((row < plan[PB]) | (row >= HALF - plan[PA]), 0, -1)


def dot(x, y, dims):
    return lax.dot_general(x, y, (dims, ((), ())), preferred_element_type=jnp.float32)


def attend(label_of, rows, results, head):
    at = pl.ds(pl.multiple_of(head * HD, HD), HD)
    columns = label_of(lax.broadcasted_iota(jnp.int32, (1, HALF), 1))
    k, v = rows[1, :, at], rows[2, :, at]
    blocks = [pl.ds(start, ROWS_STEP) for start in range(0, HALF, ROWS_STEP)]
    labels = [
        label_of(block.start + lax.broadcasted_iota(jnp.int32, (ROWS_STEP, 1), 0))
        for block in blocks
    ]
    q = [rows[0, block, at] for block in blocks]
    g = [rows[3, block, at] for block in blocks]
    scores = [dot(x, k, ((1,), (1,))) for x in q]
    masked = [jnp.where(x == columns, s, NEG_FILL) for x, s in zip(labels, scores)]
    row_max = [jnp.max(s, axis=1, keepdims=True) for s in masked]
    e = [jnp.exp2((s - m) * (SCALE * LOG2E)) for s, m in zip(masked, row_max)]
    row_total = [jnp.sum(x, axis=1, keepdims=True) for x in e]
    inverse = [jnp.where(x >= 0, 1.0 / t, 0.0) for x, t in zip(labels, row_total)]
    probs = [x * i for x, i in zip(e, inverse)]
    probs_low = [x.astype(jnp.bfloat16) for x in probs]
    attended = [dot(x, v, ((1,), (0,))) for x in probs_low]
    dprobs = [dot(x, v, ((1,), (1,))) for x in g]
    dot_term = [
        jnp.sum(x.astype(jnp.float32) * y, axis=1, keepdims=True) for x, y in zip(g, attended)
    ]
    dscore = [(x * (d - t)).astype(jnp.bfloat16) for x, d, t in zip(probs, dprobs, dot_term)]
    query_grad = [dot(x, k, ((1,), (0,))) * SCALE for x in dscore]
    for block, x, y in zip(blocks, attended, query_grad):
        results[0, block, at] = x.astype(jnp.bfloat16)
        results[1, block, at] = y.astype(jnp.bfloat16)
    key_grad = sum(dot(x, y, ((0,), (0,))) for x, y in zip(q, dscore))
    value_grad = sum(dot(x, y, ((0,), (0,))) for x, y in zip(g, probs_low))
    results[2, :, at] = (key_grad * SCALE).astype(jnp.bfloat16).T
    results[3, :, at] = value_grad.astype(jnp.bfloat16).T


def attend_in_loop(label_of, rows, results, key_total, value_total, head):
    at = pl.ds(pl.multiple_of(head * HD, HD), HD)
    columns = label_of(lax.broadcasted_iota(jnp.int32, (1, HALF), 1))
    k, v = rows[1, :, at], rows[2, :, at]
    key_total[...] = jnp.zeros_like(key_total)
    value_total[...] = jnp.zeros_like(value_total)

    def one(step, carry):
        start = pl.multiple_of(step * ROWS_STEP, ROWS_STEP)
        block = pl.ds(start, ROWS_STEP)
        labels = label_of(start + lax.broadcasted_iota(jnp.int32, (ROWS_STEP, 1), 0))
        q, g = rows[0, block, at], rows[3, block, at]
        masked = jnp.where(labels == columns, dot(q, k, ((1,), (1,))), NEG_FILL)
        row_max = jnp.max(masked, axis=1, keepdims=True)
        e = jnp.exp2((masked - row_max) * (SCALE * LOG2E))
        row_total = jnp.sum(e, axis=1, keepdims=True)
        inverse = jnp.where(labels >= 0, 1.0 / row_total, 0.0)
        probs = e * inverse
        probs_low = probs.astype(jnp.bfloat16)
        attended = dot(probs_low, v, ((1,), (0,)))
        dprobs = dot(g, v, ((1,), (1,)))
        dot_term = jnp.sum(g.astype(jnp.float32) * attended, axis=1, keepdims=True)
        dscore = (probs * (dprobs - dot_term)).astype(jnp.bfloat16)
        results[0, block, at] = attended.astype(jnp.bfloat16)
        results[1, block, at] = (dot(dscore, k, ((1,), (0,))) * SCALE).astype(jnp.bfloat16)
        key_total[...] += dot(q, dscore, ((0,), (0,)))
        value_total[...] += dot(g, probs_low, ((0,), (0,)))
        return carry

    lax.fori_loop(0, HALF // ROWS_STEP, one, 0)
    results[2, :, at] = (key_total[...] * SCALE).astype(jnp.bfloat16).T
    results[3, :, at] = value_total[...].astype(jnp.bfloat16).T


def gather_rows(q, k, v, g, peer, rows):
    for i, mine in enumerate((q, k, v, g)):
        rows[i, :OWN, :] = mine[...]
    rows[:, OWN:, :] = peer[...]


def near_kernel(plan, q, k, v, g, peer, out_0, out_1, out_2, out_3, peer_out, *scratch):
    rows, results, key_total, value_total = scratch
    gather_rows(q, k, v, g, peer, rows)

    def one(head, carry):
        labels = functools.partial(near_clips, plan)
        attend_in_loop(labels, rows, results, key_total, value_total, head)
        return carry

    lax.fori_loop(0, NEAR_HEADS, one, 0)
    for i, out in enumerate((out_0, out_1, out_2, out_3)):
        out[...] = results[i, :OWN, :]
    peer_out[...] = results[:, OWN:, :]


def cross_kernel(plan, q, k, v, g, peer, arrived, *rest):
    before, after, (leaving, rows, results) = rest[:5], rest[5:10], rest[10:]
    step = pl.program_id(0)
    far = plan[FAR]
    labels = functools.partial(cross_clip, plan)

    def place(frame):
        return pl.ds(pl.multiple_of(local_row(plan, plan[FARROW] + FPT * frame), FPT), FPT)

    def near_rows(start):
        row = local_row(plan, start + lax.broadcasted_iota(jnp.int32, (OWN, HD), 0))
        return (row >= plan[NEARROW]) & (row < plan[NEARROW] + FPT * plan[NEAR])

    def one(head, carry):
        at = pl.ds(pl.multiple_of(head * HD, HD), HD)
        order = (plan[PAIR] + step) * 2 + head - plan[FIRST]
        here = (order >= 0) & (order < plan[COUNT])

        def take(frame, carry):
            rows[:, place(frame), at] = arrived[order * far + frame]
            return carry

        def give(frame, carry):
            leaving[order * far + frame] = results[:, place(frame), at]
            return carry

        @pl.when(here)
        def _():
            lax.fori_loop(0, far, take, 0)
            attend(labels, rows, results, head)
            lax.fori_loop(0, far, give, 0)
            own_near, peer_near = near_rows(0), near_rows(OWN)
            for i in range(4):
                after[i][:, at] = jnp.where(own_near, results[i, :OWN, at], before[i][:, at])
                after[4][i, :, at] = jnp.where(
                    peer_near, results[i, OWN:, at], before[4][i, :, at]
                )

        @pl.when(jnp.logical_not(here))
        def _():
            for i in range(4):
                after[i][:, at] = before[i][:, at]
                after[4][i, :, at] = before[4][i, :, at]

        return carry

    @pl.when((step < plan[PAIRS]) | (step == 0))
    def _():
        gather_rows(q, k, v, g, peer, rows)
        lax.fori_loop(0, 2, one, 0)


def head_specs(heads, at):
    steps, width = MINE // heads, heads * HD
    own = [pl.BlockSpec((OWN, width), lambda i, plan: (0, plan[CORE] * steps + at(i, plan)))] * 4
    half = pl.BlockSpec((4, OWN, width), lambda i, plan: (0, 0, at(i, plan)))
    return own, half


def head_scratch(heads):
    return [pltpu.VMEM((4, HALF, heads * HD), jnp.bfloat16)] * 2


PARAMS = pltpu.CompilerParams(vmem_limit_bytes=40 * 1024 * 1024)
HALF_SHAPE = jax.ShapeDtypeStruct((4, OWN, COLS), jnp.bfloat16)
OUT_SHAPES = [jax.ShapeDtypeStruct((OWN, HEADS * HD), jnp.bfloat16)] * 4


def near_call(plan, arrays, peer):
    own, half = head_specs(NEAR_HEADS, lambda i, plan: i)
    return pl.pallas_call(
        near_kernel,
        grid_spec=pltpu.PrefetchScalarGridSpec(
            num_scalar_prefetch=1,
            grid=(MINE // NEAR_HEADS,),
            in_specs=own + [half],
            out_specs=own + [half],
            scratch_shapes=head_scratch(NEAR_HEADS) + [pltpu.VMEM((HD, HALF), jnp.float32)] * 2,
        ),
        out_shape=OUT_SHAPES + [HALF_SHAPE],
        compiler_params=PARAMS,
        name="near_clips",
    )(plan, *arrays, peer)


def cross_call(plan, arrays, peer, arrived, results):
    own, half = head_specs(
        2, lambda i, plan: plan[PAIR] + jnp.minimum(i, jnp.maximum(plan[PAIRS], 1) - 1)
    )
    whole = pl.BlockSpec(arrived.shape, lambda i, plan: (0, 0, 0, 0))
    return pl.pallas_call(
        cross_kernel,
        grid_spec=pltpu.PrefetchScalarGridSpec(
            num_scalar_prefetch=1,
            grid=(MINE // 2,),
            in_specs=own + [half, whole] + own + [half],
            out_specs=own + [half, whole],
            scratch_shapes=head_scratch(2),
        ),
        out_shape=OUT_SHAPES + [HALF_SHAPE, jax.ShapeDtypeStruct(arrived.shape, jnp.bfloat16)],
        input_output_aliases={7 + i: i for i in range(5)},
        compiler_params=PARAMS,
        name="cross_clip",
    )(plan, *arrays, peer, arrived, *results)


ANY = pl.BlockSpec(memory_space=pl.ANY)


def near_slots(plan, body):
    near = plan[NEAR]

    def one_head(head, carry):
        def one(frame, carry):
            row = pl.multiple_of(plan[NEARROW] + FPT * frame, FPT)
            body(head * near + frame, plan[AWAY] + head, row)
            return carry

        return lax.fori_loop(0, near, one, carry)

    lax.fori_loop(0, plan[GONE], one_head, 0)


SMEM = pl.BlockSpec(memory_space=pltpu.SMEM)
VMEM = pl.BlockSpec(memory_space=pltpu.VMEM)


SLOTS_SHAPE = jax.ShapeDtypeStruct((SLOTS[0], 4, FPT, HD), jnp.bfloat16)


def first_kernel(place, frames_in, offsets_in, q, k, v, g, plan, mine, give, *scratch):
    frames, offsets, rows, table_sems, sems = scratch
    tables = [
        pltpu.make_async_copy(frames_in, frames, table_sems.at[0]),
        pltpu.make_async_copy(offsets_in, offsets, table_sems.at[1]),
    ]
    for c in tables:
        c.start()
    for c in tables:
        c.wait()
    fill_plan(plan, place, frames, offsets)
    own = plan[CORE] * OWN
    begin = jnp.clip(plan[NEARROW] - own, 0, OWN) >> FPT_BITS
    end = jnp.clip(plan[NEARROW] + FPT * plan[NEAR] - own, 0, OWN) >> FPT_BITS

    def copies(frame):
        at = pl.ds(pl.multiple_of(FPT * frame, FPT), FPT)
        return [
            pltpu.make_async_copy(x.at[at, :], rows.at[i, at, :], sems.at[frame, i])
            for i, x in enumerate((q, k, v, g))
        ]

    def start(frame, carry):
        for c in copies(frame):
            c.start()
        return carry

    def wait(frame, carry):
        for c in copies(frame):
            c.wait()
        return carry

    lax.fori_loop(begin, end, start, 0)
    mine[...] = jnp.zeros_like(mine)
    give[...] = jnp.zeros_like(give)
    lax.fori_loop(begin, end, wait, 0)

    def body(slot, head, row):
        @pl.when((row >= OWN) == (plan[CORE] == 1))
        def _():
            at = pl.ds(pl.multiple_of(row & (OWN - 1), FPT), FPT)
            for out, core in ((mine, plan[CORE]), (give, 1 - plan[CORE])):
                col = pl.ds(pl.multiple_of((core * MINE + head) * HD, HD), HD)
                out[slot] = rows[:, at, col]

    near_slots(plan, body)


def first_call(place, frames, offsets, arrays):
    return pl.pallas_call(
        first_kernel,
        in_specs=[SMEM] + [ANY] * 6,
        out_specs=[SMEM, VMEM, VMEM],
        out_shape=[jax.ShapeDtypeStruct((BRANCH + 1,), jnp.int32), SLOTS_SHAPE, SLOTS_SHAPE],
        scratch_shapes=[
            pltpu.SMEM(frames.shape, jnp.int32),
            pltpu.SMEM(offsets.shape, jnp.int32),
            pltpu.VMEM((4, OWN, HEADS * HD), jnp.bfloat16),
            pltpu.SemaphoreType.DMA((2,)),
            pltpu.SemaphoreType.DMA((OWN // FPT, 4)),
        ],
        compiler_params=PARAMS,
        name="first_blocks",
    )(place, frames, offsets, *arrays)


def split_kernel(place, q, k, v, g, out, sems):
    col = pl.ds(pl.multiple_of((1 - (place[1] & 1)) * COLS, COLS), COLS)
    copies = [
        pltpu.make_async_copy(x.at[:, col], out.at[i], sems.at[i])
        for i, x in enumerate((q, k, v, g))
    ]
    for c in copies:
        c.start()
    for c in copies:
        c.wait()


def split_call(place, arrays):
    return pl.pallas_call(
        split_kernel,
        in_specs=[SMEM] + [ANY] * 4,
        out_specs=VMEM,
        out_shape=HALF_SHAPE,
        scratch_shapes=[pltpu.SemaphoreType.DMA((4,))],
        compiler_params=PARAMS,
        name="split_heads",
    )(place, *arrays)


def join_kernel(plan, other, *rest):
    for i, out in enumerate(rest[4:]):
        out[...] = other[i]


def join_call(plan, other, outs):
    width = COLS // JOIN_STEPS
    block = pl.BlockSpec((OWN, width), lambda i, plan: (0, (1 - plan[CORE]) * JOIN_STEPS + i))
    return pl.pallas_call(
        join_kernel,
        grid_spec=pltpu.PrefetchScalarGridSpec(
            num_scalar_prefetch=1,
            grid=(JOIN_STEPS,),
            in_specs=[pl.BlockSpec((4, OWN, width), lambda i, plan: (0, 0, i))] + [ANY] * 4,
            out_specs=[block] * 4,
        ),
        out_shape=OUT_SHAPES,
        input_output_aliases={2 + i: i for i in range(4)},
        compiler_params=PARAMS,
        name="join_halves",
    )(plan, other, *outs)


def unpack_kernel(plan, mine, other, *rest):
    outs, sems = rest[4:8], rest[8]

    def each(act):
        def body(slot, head, row):
            @pl.when((row >= OWN) == (plan[CORE] == 1))
            def _():
                at = pl.ds(pl.multiple_of(row & (OWN - 1), FPT), FPT)
                for j, back in enumerate((mine, other)):
                    core = plan[CORE] if j == 0 else 1 - plan[CORE]
                    col = pl.ds(pl.multiple_of((core * MINE + head) * HD, HD), HD)
                    for i, out in enumerate(outs):
                        act(
                            pltpu.make_async_copy(
                                back.at[slot, i], out.at[at, col], sems.at[slot, j, i]
                            )
                        )

        near_slots(plan, body)

    each(lambda c: c.start())
    each(lambda c: c.wait())


def unpack_call(plan, mine, other, outs):
    return pl.pallas_call(
        unpack_kernel,
        in_specs=[SMEM, VMEM, VMEM] + [ANY] * 4,
        out_specs=[ANY] * 4,
        out_shape=OUT_SHAPES,
        input_output_aliases={3: 0, 4: 1, 5: 2, 6: 3},
        scratch_shapes=[pltpu.SemaphoreType.DMA((mine.shape[0], 2, 4))],
        compiler_params=PARAMS,
        name="unpack_cross",
    )(plan, mine, other, *outs)


OTHER_CORE = [(i, i ^ 1) for i in range(4)]
OTHER_CHIP = [(i, i ^ 2) for i in range(4)]


def branch_in(slots):
    def run(plan, arrays, sent, mine, got):
        if slots:
            arrived = lax.ppermute(mine[:slots] + got[:slots], "ulysses", OTHER_CHIP)
        peer = lax.ppermute(sent, "ulysses", OTHER_CORE)
        results = near_call(plan, arrays, peer)
        if not slots:
            return results, peer, jnp.zeros(SLOTS_SHAPE.shape, jnp.bfloat16)
        results, arrived = lax.optimization_barrier((results, arrived))
        return results, peer, pad_slots(arrived)

    return run


def branch_out(slots):
    def run(plan, results, leaving):
        if slots:
            returned = lax.ppermute(leaving[:slots], "ulysses", OTHER_CHIP)
        other = lax.ppermute(results[4], "ulysses", OTHER_CORE)
        outs = join_call(plan, other, results[:4])
        if not slots:
            return outs, jnp.zeros(SLOTS_SHAPE.shape, jnp.bfloat16)
        outs, returned = lax.optimization_barrier((outs, returned))
        return outs, pad_slots(returned)

    return run


def pad_slots(blocks):
    return jnp.pad(blocks, ((0, SLOTS[0] - blocks.shape[0]), (0, 0), (0, 0), (0, 0)))


def shards(queries, key_rows, values, out_grad, frames, offsets):
    place = jnp.stack([lax.axis_index("dp"), lax.axis_index("ulysses")]).astype(jnp.int32)
    arrays = (queries, key_rows, values, out_grad)
    plan, mine, give = first_call(place, frames.T, offsets.T, arrays)
    got = lax.ppermute(give, "ulysses", OTHER_CORE)
    sent = split_call(place, arrays)
    branch = plan[BRANCH]
    results, peer, arrived = lax.switch(
        branch, [branch_in(n) for n in SLOTS], plan, arrays, sent, mine, got
    )
    *results, leaving = cross_call(plan, arrays, peer, arrived, results)
    outs, returned = lax.switch(
        branch, [branch_out(n) for n in SLOTS], plan, results, leaving
    )
    returned_other = lax.ppermute(returned, "ulysses", OTHER_CORE)
    return tuple(unpack_call(plan, returned, returned_other, outs))


def solution(mesh):
    rows = P(("dp", "ulysses"), None)
    return jax.shard_map(
        shards,
        mesh=mesh,
        in_specs=(rows, rows, rows, rows, P(), P()),
        out_specs=(rows, rows, rows, rows),
        check_vma=False,
    )
```

```python
import functools
import math

import jax
import jax.numpy as jnp
from jax import lax
from jax.experimental import pallas as pl
from jax.experimental.pallas import tpu as pltpu
from jax.sharding import PartitionSpec as P

HEADS = 20
HD = 128
FPT = 64
FPT_BITS = 6
HALF = 512
OWN = 256
MINE = 10
COLS = MINE * HD
NEG_FILL = -1e30
ANY = pl.BlockSpec(memory_space=pl.ANY)
SMEM = pl.BlockSpec(memory_space=pltpu.SMEM)
VMEM = pl.BlockSpec(memory_space=pltpu.VMEM)
SCALE = 1.0 / math.sqrt(HD)
LOG2E = math.log2(math.e)
ROWS_STEP = 256
JOIN_STEPS = 5
NEAR_HEADS = 2

SLOTS = (20, 18, 16, 15, 12, 10, 8, 0)


CORE, B0, E0, B1, E1, PA, PB, FIRST, COUNT, NEAR, FAR, NEARROW, FARROW, AWAY, GONE, PAIR, PAIRS, BRANCH = range(18)


def split_heads(a, b):
    best, heads = jnp.maximum(a, b * (MINE - 1)), 1
    for h in range(2, MINE):
        cost = jnp.maximum(a * h, b * (MINE - h))
        heads = jnp.where(cost < best, h, heads)
        best = jnp.minimum(cost, best)
    return heads, jnp.where((a > 0) & (b > 0), best, 0)


def fill_plan(plan, place, tables):
    group, core, high = place[0], place[1] & 1, place[1] >> 1
    base = high * HALF
    a = b = 0
    for i, (begin_at, end_at) in enumerate(((B0, E0), (B1, E1))):
        begin = tables[2 + i, group]
        end = begin + tables[i, group] * FPT
        crosses = (begin < HALF) & (end > HALF)
        a = jnp.where(crosses, (HALF - begin) >> FPT_BITS, a)
        b = jnp.where(crosses, (end - HALF) >> FPT_BITS, b)
        plan[begin_at] = jnp.where(crosses, 0, begin - base)
        plan[end_at] = jnp.where(crosses, 0, end - base)
    h, cost = split_heads(a, b)
    branch = 0
    for i, n in enumerate(SLOTS[1:]):
        branch = jnp.where(cost <= n, i + 1, branch)
    second = high == 1
    plan[CORE] = core
    plan[PA] = FPT * a
    plan[PB] = FPT * b
    plan[FIRST] = jnp.where(second, 0, h)
    plan[COUNT] = jnp.where(cost == 0, 0, jnp.where(second, h, MINE - h))
    plan[GONE] = jnp.where(cost == 0, 0, jnp.where(second, MINE - h, h))
    plan[NEAR] = jnp.where(second, b, a)
    plan[FAR] = jnp.where(second, a, b)
    plan[NEARROW] = jnp.where(second, 0, HALF - FPT * a)
    plan[FARROW] = jnp.where(second, HALF - FPT * a, 0)
    plan[PAIR] = jnp.where(second, 0, h >> 1)
    plan[PAIRS] = jnp.where(cost == 0, 0, jnp.where(second, (h + 1) >> 1, MINE // 2 - (h >> 1)))
    plan[AWAY] = jnp.where(second, h, 0)
    plan[BRANCH] = branch


def local_row(plan, position):
    return (position + OWN * plan[CORE]) & (HALF - 1)


def near_clips(plan, position):
    row = local_row(plan, position)
    first = (row >= plan[B0]) & (row < plan[E0])
    second = (row >= plan[B1]) & (row < plan[E1])
    return jnp.where(first, 0, jnp.where(second, 1, -1))


def cross_clip(plan, position):
    row = local_row(plan, position)
    return jnp.where((row < plan[PB]) | (row >= HALF - plan[PA]), 0, -1)


def dot(x, y, dims):
    return lax.dot_general(x, y, (dims, ((), ())), preferred_element_type=jnp.float32)


def attend(label_of, rows, results, head):
    at = pl.ds(pl.multiple_of(head * HD, HD), HD)
    columns = label_of(lax.broadcasted_iota(jnp.int32, (1, HALF), 1))
    k, v = rows[1, :, at], rows[2, :, at]
    blocks = [pl.ds(start, ROWS_STEP) for start in range(0, HALF, ROWS_STEP)]
    labels = [
        label_of(block.start + lax.broadcasted_iota(jnp.int32, (ROWS_STEP, 1), 0))
        for block in blocks
    ]
    q = [rows[0, block, at] for block in blocks]
    g = [rows[3, block, at] for block in blocks]
    scores = [dot(x, k, ((1,), (1,))) for x in q]
    masked = [jnp.where(x == columns, s, NEG_FILL) for x, s in zip(labels, scores)]
    row_max = [jnp.max(s, axis=1, keepdims=True) for s in masked]
    e = [jnp.exp2((s - m) * (SCALE * LOG2E)) for s, m in zip(masked, row_max)]
    row_total = [jnp.sum(x, axis=1, keepdims=True) for x in e]
    inverse = [jnp.where(x >= 0, 1.0 / t, 0.0) for x, t in zip(labels, row_total)]
    probs = [x * i for x, i in zip(e, inverse)]
    probs_low = [x.astype(jnp.bfloat16) for x in probs]
    attended = [dot(x, v, ((1,), (0,))) for x in probs_low]
    dprobs = [dot(x, v, ((1,), (1,))) for x in g]
    dot_term = [
        jnp.sum(x.astype(jnp.float32) * y, axis=1, keepdims=True) for x, y in zip(g, attended)
    ]
    scaled = [x * (i * SCALE) for x, i in zip(e, inverse)]
    dscore = [(x * (d - t)).astype(jnp.bfloat16) for x, d, t in zip(scaled, dprobs, dot_term)]
    query_grad = [dot(x, k, ((1,), (0,))) for x in dscore]
    for block, x, y in zip(blocks, attended, query_grad):
        results[0, block, at] = x.astype(jnp.bfloat16)
        results[1, block, at] = y.astype(jnp.bfloat16)
    key_grad = sum(dot(x, y, ((0,), (0,))) for x, y in zip(q, dscore))
    value_grad = sum(dot(x, y, ((0,), (0,))) for x, y in zip(g, probs_low))
    results[2, :, at] = key_grad.astype(jnp.bfloat16).T
    results[3, :, at] = value_grad.astype(jnp.bfloat16).T


def attend_in_loop(label_of, rows, results, key_total, value_total, head):
    at = pl.ds(pl.multiple_of(head * HD, HD), HD)
    columns = label_of(lax.broadcasted_iota(jnp.int32, (1, HALF), 1))
    k, v = rows[1, :, at], rows[2, :, at]
    key_total[...] = jnp.zeros_like(key_total)
    value_total[...] = jnp.zeros_like(value_total)

    def one(step, carry):
        start = pl.multiple_of(step * ROWS_STEP, ROWS_STEP)
        block = pl.ds(start, ROWS_STEP)
        labels = label_of(start + lax.broadcasted_iota(jnp.int32, (ROWS_STEP, 1), 0))
        q, g = rows[0, block, at], rows[3, block, at]
        masked = jnp.where(labels == columns, dot(q, k, ((1,), (1,))), NEG_FILL)
        row_max = jnp.max(masked, axis=1, keepdims=True)
        e = jnp.exp2((masked - row_max) * (SCALE * LOG2E))
        row_total = jnp.sum(e, axis=1, keepdims=True)
        inverse = jnp.where(labels >= 0, 1.0 / row_total, 0.0)
        probs = e * inverse
        probs_low = probs.astype(jnp.bfloat16)
        attended = dot(probs_low, v, ((1,), (0,)))
        dprobs = dot(g, v, ((1,), (1,)))
        dot_term = jnp.sum(g.astype(jnp.float32) * attended, axis=1, keepdims=True)
        dscore = (e * (inverse * SCALE) * (dprobs - dot_term)).astype(jnp.bfloat16)
        results[0, block, at] = attended.astype(jnp.bfloat16)
        results[1, block, at] = dot(dscore, k, ((1,), (0,))).astype(jnp.bfloat16)
        key_total[...] += dot(q, dscore, ((0,), (0,)))
        value_total[...] += dot(g, probs_low, ((0,), (0,)))
        return carry

    lax.fori_loop(0, HALF // ROWS_STEP, one, 0)
    results[2, :, at] = key_total[...].astype(jnp.bfloat16).T
    results[3, :, at] = value_total[...].astype(jnp.bfloat16).T


def gather_rows(q, k, v, g, peer, rows):
    for i, mine in enumerate((q, k, v, g)):
        rows[i, :OWN, :] = mine[...]
    rows[:, OWN:, :] = peer[...]


def near_kernel(plan, q, k, v, g, peer, out_0, out_1, out_2, out_3, peer_out, *scratch):
    rows, results, key_total, value_total = scratch
    gather_rows(q, k, v, g, peer, rows)

    def one(head, carry):
        labels = functools.partial(near_clips, plan)
        attend_in_loop(labels, rows, results, key_total, value_total, head)
        return carry

    lax.fori_loop(0, NEAR_HEADS, one, 0)
    for i, out in enumerate((out_0, out_1, out_2, out_3)):
        out[...] = results[i, :OWN, :]
    peer_out[...] = results[:, OWN:, :]


def cross_kernel(plan, q, k, v, g, peer, arrived, *rest):
    before, after, (leaving, rows, results) = rest[:5], rest[5:10], rest[10:]
    step = pl.program_id(0)
    far = plan[FAR]
    labels = functools.partial(cross_clip, plan)

    def place(frame):
        return pl.ds(pl.multiple_of(local_row(plan, plan[FARROW] + FPT * frame), FPT), FPT)

    def near_rows(start):
        row = local_row(plan, start + lax.broadcasted_iota(jnp.int32, (OWN, HD), 0))
        return (row >= plan[NEARROW]) & (row < plan[NEARROW] + FPT * plan[NEAR])

    def one(head, carry):
        at = pl.ds(pl.multiple_of(head * HD, HD), HD)
        order = (plan[PAIR] + step) * 2 + head - plan[FIRST]
        here = (order >= 0) & (order < plan[COUNT])

        def take(frame, carry):
            rows[:, place(frame), at] = arrived[order * far + frame]
            return carry

        def give(frame, carry):
            leaving[order * far + frame] = results[:, place(frame), at]
            return carry

        @pl.when(here)
        def _():
            lax.fori_loop(0, far, take, 0)
            attend(labels, rows, results, head)
            lax.fori_loop(0, far, give, 0)
            own_near, peer_near = near_rows(0), near_rows(OWN)
            for i in range(4):
                after[i][:, at] = jnp.where(own_near, results[i, :OWN, at], before[i][:, at])
                after[4][i, :, at] = jnp.where(
                    peer_near, results[i, OWN:, at], before[4][i, :, at]
                )

        @pl.when(jnp.logical_not(here))
        def _():
            for i in range(4):
                after[i][:, at] = before[i][:, at]
                after[4][i, :, at] = before[4][i, :, at]

        return carry

    @pl.when((step < plan[PAIRS]) | (step == 0))
    def _():
        gather_rows(q, k, v, g, peer, rows)
        lax.fori_loop(0, 2, one, 0)


def head_specs(heads, at):
    steps, width = MINE // heads, heads * HD
    own = [pl.BlockSpec((OWN, width), lambda i, plan: (0, plan[CORE] * steps + at(i, plan)))] * 4
    half = pl.BlockSpec((4, OWN, width), lambda i, plan: (0, 0, at(i, plan)))
    return own, half


def head_scratch(heads):
    return [pltpu.VMEM((4, HALF, heads * HD), jnp.bfloat16)] * 2


PARAMS = pltpu.CompilerParams(vmem_limit_bytes=40 * 1024 * 1024)
HALF_SHAPE = jax.ShapeDtypeStruct((4, OWN, COLS), jnp.bfloat16)
OUT_SHAPES = [jax.ShapeDtypeStruct((OWN, HEADS * HD), jnp.bfloat16)] * 4


def near_call(plan, arrays, peer):
    own, half = head_specs(NEAR_HEADS, lambda i, plan: i)
    return pl.pallas_call(
        near_kernel,
        grid_spec=pltpu.PrefetchScalarGridSpec(
            num_scalar_prefetch=1,
            grid=(MINE // NEAR_HEADS,),
            in_specs=own + [half],
            out_specs=own + [half],
            scratch_shapes=head_scratch(NEAR_HEADS) + [pltpu.VMEM((HD, HALF), jnp.float32)] * 2,
        ),
        out_shape=OUT_SHAPES + [HALF_SHAPE],
        compiler_params=PARAMS,
        name="near_clips",
    )(plan, *arrays, peer)


def cross_call(plan, arrays, peer, arrived, results):
    own, half = head_specs(
        2, lambda i, plan: plan[PAIR] + jnp.minimum(i, jnp.maximum(plan[PAIRS], 1) - 1)
    )
    whole = pl.BlockSpec(arrived.shape, lambda i, plan: (0, 0, 0, 0))
    return pl.pallas_call(
        cross_kernel,
        grid_spec=pltpu.PrefetchScalarGridSpec(
            num_scalar_prefetch=1,
            grid=(MINE // 2,),
            in_specs=own + [half, whole] + own + [half],
            out_specs=own + [half, whole],
            scratch_shapes=head_scratch(2),
        ),
        out_shape=OUT_SHAPES + [HALF_SHAPE, jax.ShapeDtypeStruct(arrived.shape, jnp.bfloat16)],
        input_output_aliases={7 + i: i for i in range(5)},
        compiler_params=PARAMS,
        name="cross_clip",
    )(plan, *arrays, peer, arrived, *results)


def near_slots(plan, body):
    near = plan[NEAR]

    def one_head(head, carry):
        def one(frame, carry):
            row = pl.multiple_of(plan[NEARROW] + FPT * frame, FPT)
            body(head * near + frame, plan[AWAY] + head, row)
            return carry

        return lax.fori_loop(0, near, one, carry)

    lax.fori_loop(0, plan[GONE], one_head, 0)


SLOTS_SHAPE = jax.ShapeDtypeStruct((SLOTS[0], 4, FPT, HD), jnp.bfloat16)


def first_kernel(place, tables, q, k, v, g, plan, mine, give):
    fill_plan(plan, place, tables)
    mine[...] = jnp.zeros_like(mine)
    give[...] = jnp.zeros_like(give)

    def body(slot, head, row):
        @pl.when((row >= OWN) == (plan[CORE] == 1))
        def _():
            at = pl.ds(pl.multiple_of(row & (OWN - 1), FPT), FPT)
            for out, core in ((mine, plan[CORE]), (give, 1 - plan[CORE])):
                col = pl.ds(pl.multiple_of((core * MINE + head) * HD, HD), HD)
                for i, x in enumerate((q, k, v, g)):
                    out[slot, i] = x[at, col]

    near_slots(plan, body)


def first_call(place, tables, arrays):
    return pl.pallas_call(
        first_kernel,
        in_specs=[SMEM] * 2 + [VMEM] * 4,
        out_specs=[SMEM, VMEM, VMEM],
        out_shape=[jax.ShapeDtypeStruct((BRANCH + 1,), jnp.int32), SLOTS_SHAPE, SLOTS_SHAPE],
        compiler_params=PARAMS,
        name="first_blocks",
    )(place, tables, *arrays)


def split_kernel(place, q, k, v, g, out, sems):
    col = pl.ds(pl.multiple_of((1 - (place[1] & 1)) * COLS, COLS), COLS)
    copies = [
        pltpu.make_async_copy(x.at[:, col], out.at[i], sems.at[i])
        for i, x in enumerate((q, k, v, g))
    ]
    for c in copies:
        c.start()
    for c in copies:
        c.wait()


def split_call(place, arrays):
    return pl.pallas_call(
        split_kernel,
        in_specs=[SMEM] + [ANY] * 4,
        out_specs=VMEM,
        out_shape=HALF_SHAPE,
        scratch_shapes=[pltpu.SemaphoreType.DMA((4,))],
        compiler_params=PARAMS,
        name="split_heads",
    )(place, *arrays)


def join_kernel(plan, other, *rest):
    for i, out in enumerate(rest[4:]):
        out[...] = other[i]


def join_call(plan, other, outs):
    width = COLS // JOIN_STEPS
    block = pl.BlockSpec((OWN, width), lambda i, plan: (0, (1 - plan[CORE]) * JOIN_STEPS + i))
    return pl.pallas_call(
        join_kernel,
        grid_spec=pltpu.PrefetchScalarGridSpec(
            num_scalar_prefetch=1,
            grid=(JOIN_STEPS,),
            in_specs=[pl.BlockSpec((4, OWN, width), lambda i, plan: (0, 0, i))] + [ANY] * 4,
            out_specs=[block] * 4,
        ),
        out_shape=OUT_SHAPES,
        input_output_aliases={2 + i: i for i in range(4)},
        compiler_params=PARAMS,
        name="join_halves",
    )(plan, other, *outs)


def unpack_kernel(plan, mine, other, *rest):
    outs, sems = rest[4:8], rest[8]

    def each(act):
        def body(slot, head, row):
            @pl.when((row >= OWN) == (plan[CORE] == 1))
            def _():
                at = pl.ds(pl.multiple_of(row & (OWN - 1), FPT), FPT)
                for j, back in enumerate((mine, other)):
                    core = plan[CORE] if j == 0 else 1 - plan[CORE]
                    col = pl.ds(pl.multiple_of((core * MINE + head) * HD, HD), HD)
                    for i, out in enumerate(outs):
                        act(
                            pltpu.make_async_copy(
                                back.at[slot, i], out.at[at, col], sems.at[slot, j, i]
                            )
                        )

        near_slots(plan, body)

    each(lambda c: c.start())
    each(lambda c: c.wait())


def unpack_call(plan, mine, other, outs):
    return pl.pallas_call(
        unpack_kernel,
        in_specs=[SMEM, VMEM, VMEM] + [ANY] * 4,
        out_specs=[ANY] * 4,
        out_shape=OUT_SHAPES,
        input_output_aliases={3: 0, 4: 1, 5: 2, 6: 3},
        scratch_shapes=[pltpu.SemaphoreType.DMA((mine.shape[0], 2, 4))],
        compiler_params=PARAMS,
        name="unpack_cross",
    )(plan, mine, other, *outs)


OTHER_CORE = [(i, i ^ 1) for i in range(4)]
OTHER_CHIP = [(i, i ^ 2) for i in range(4)]


def branch_in(slots):
    def run(plan, arrays, peer, mine, got):
        if slots:
            arrived = lax.ppermute(mine[:slots] + got[:slots], "ulysses", OTHER_CHIP)
        results = near_call(plan, arrays, peer)
        if not slots:
            return results, jnp.zeros(SLOTS_SHAPE.shape, jnp.bfloat16)
        results, arrived = lax.optimization_barrier((results, arrived))
        return results, pad_slots(arrived)

    return run


def branch_out(slots):
    def run(plan, results, leaving):
        if slots:
            returned = lax.ppermute(leaving[:slots], "ulysses", OTHER_CHIP)
        other = lax.ppermute(results[4], "ulysses", OTHER_CORE)
        outs = join_call(plan, other, results[:4])
        if not slots:
            return outs, jnp.zeros(SLOTS_SHAPE.shape, jnp.bfloat16)
        outs, returned = lax.optimization_barrier((outs, returned))
        return outs, pad_slots(returned)

    return run


def pad_slots(blocks):
    return jnp.pad(blocks, ((0, SLOTS[0] - blocks.shape[0]), (0, 0), (0, 0), (0, 0)))


def shards(queries, key_rows, values, out_grad, frames, offsets):
    place = jnp.stack([lax.axis_index("dp"), lax.axis_index("ulysses")]).astype(jnp.int32)
    arrays = (queries, key_rows, values, out_grad)
    sent = split_call(place, arrays)
    peer = lax.ppermute(sent, "ulysses", OTHER_CORE)
    tables = jnp.concatenate([frames.T, offsets.T])
    sent, tables, place = lax.optimization_barrier((sent, tables, place))
    plan, mine, give = first_call(place, tables, arrays)
    got = lax.ppermute(give, "ulysses", OTHER_CORE)
    branch = plan[BRANCH]
    results, arrived = lax.switch(
        branch, [branch_in(n) for n in SLOTS], plan, arrays, peer, mine, got
    )
    *results, leaving = cross_call(plan, arrays, peer, arrived, results)
    outs, returned = lax.switch(
        branch, [branch_out(n) for n in SLOTS], plan, results, leaving
    )
    returned_other = lax.ppermute(returned, "ulysses", OTHER_CORE)
    return tuple(unpack_call(plan, returned, returned_other, outs))


def solution(mesh):
    rows = P(("dp", "ulysses"), None)
    return jax.shard_map(
        shards,
        mesh=mesh,
        in_specs=(rows, rows, rows, rows, P(), P()),
        out_specs=(rows, rows, rows, rows),
        check_vma=False,
    )
```

```python
import functools
import math

import jax
import jax.numpy as jnp
from jax import lax
from jax.experimental import pallas as pl
from jax.experimental.pallas import tpu as pltpu
from jax.sharding import PartitionSpec as P

HEADS = 20
HD = 128
FPT = 64
FPT_BITS = 6
HALF = 512
OWN = 256
MINE = 10
COLS = MINE * HD
NEG_FILL = -1e30
ANY = pl.BlockSpec(memory_space=pl.ANY)
SMEM = pl.BlockSpec(memory_space=pltpu.SMEM)
VMEM = pl.BlockSpec(memory_space=pltpu.VMEM)
SCALE = 1.0 / math.sqrt(HD)
LOG2E = math.log2(math.e)
ROWS_STEP = 256
JOIN_STEPS = 5
NEAR_HEADS = 2

SLOTS = (20, 18, 15, 12, 10, 0)
LATE_SLOTS = (15, 10)


CORE, B0, E0, B1, E1, PA, PB, FIRST, COUNT, NEAR, FAR, NEARROW, FARROW, AWAY, GONE, PAIR, PAIRS, BRANCH, BRANCH_IN = range(19)


def split_heads(a, b):
    best, heads = jnp.maximum(a, b * (MINE - 1)), 1
    for h in range(2, MINE):
        cost = jnp.maximum(a * h, b * (MINE - h))
        heads = jnp.where(cost < best, h, heads)
        best = jnp.minimum(cost, best)
    return heads, jnp.where((a > 0) & (b > 0), best, 0)


def crossing(tables, group):
    a = b = 0
    for i in range(2):
        begin = tables[2 + i, group]
        end = begin + tables[i, group] * FPT
        crosses = (begin < HALF) & (end > HALF)
        a = jnp.where(crosses, (HALF - begin) >> FPT_BITS, a)
        b = jnp.where(crosses, (end - HALF) >> FPT_BITS, b)
    return (a, b, *split_heads(a, b))


def place_in(choices, cost):
    found = 0
    for i, n in enumerate(choices[1:]):
        found = jnp.where(cost <= n, i + 1, found)
    return found


def fill_plan(plan, place, tables):
    group, core, high = place[0], place[1] & 1, place[1] >> 1
    base = high * HALF
    for i, (begin_at, end_at) in enumerate(((B0, E0), (B1, E1))):
        begin = tables[2 + i, group]
        end = begin + tables[i, group] * FPT
        crosses = (begin < HALF) & (end > HALF)
        plan[begin_at] = jnp.where(crosses, 0, begin - base)
        plan[end_at] = jnp.where(crosses, 0, end - base)
    a, b, h, cost = crossing(tables, group)
    other = crossing(tables, group ^ 2)[3]
    late = (cost > 0) & (cost <= LATE_SLOTS[0]) & ((other > cost) | ((other == cost) & ((group & 2) == 2)))
    branch = place_in(SLOTS, cost)
    plan[BRANCH_IN] = jnp.where(late, len(SLOTS) + place_in(LATE_SLOTS, cost), branch)
    second = high == 1
    plan[CORE] = core
    plan[PA] = FPT * a
    plan[PB] = FPT * b
    plan[FIRST] = jnp.where(second, 0, h)
    plan[COUNT] = jnp.where(cost == 0, 0, jnp.where(second, h, MINE - h))
    plan[GONE] = jnp.where(cost == 0, 0, jnp.where(second, MINE - h, h))
    plan[NEAR] = jnp.where(second, b, a)
    plan[FAR] = jnp.where(second, a, b)
    plan[NEARROW] = jnp.where(second, 0, HALF - FPT * a)
    plan[FARROW] = jnp.where(second, HALF - FPT * a, 0)
    plan[PAIR] = jnp.where(second, 0, h >> 1)
    plan[PAIRS] = jnp.where(cost == 0, 0, jnp.where(second, (h + 1) >> 1, MINE // 2 - (h >> 1)))
    plan[AWAY] = jnp.where(second, h, 0)
    plan[BRANCH] = branch


def local_row(plan, position):
    return (position + OWN * plan[CORE]) & (HALF - 1)


def near_clips(plan, position):
    row = local_row(plan, position)
    first = (row >= plan[B0]) & (row < plan[E0])
    second = (row >= plan[B1]) & (row < plan[E1])
    return jnp.where(first, 0, jnp.where(second, 1, -1))


def cross_clip(plan, position):
    row = local_row(plan, position)
    return jnp.where((row < plan[PB]) | (row >= HALF - plan[PA]), 0, -1)


def dot(x, y, dims):
    return lax.dot_general(x, y, (dims, ((), ())), preferred_element_type=jnp.float32)


def attend(label_of, rows, results, head):
    at = pl.ds(pl.multiple_of(head * HD, HD), HD)
    columns = label_of(lax.broadcasted_iota(jnp.int32, (1, HALF), 1))
    k, v = rows[1, :, at], rows[2, :, at]
    blocks = [pl.ds(start, ROWS_STEP) for start in range(0, HALF, ROWS_STEP)]
    labels = [
        label_of(block.start + lax.broadcasted_iota(jnp.int32, (ROWS_STEP, 1), 0))
        for block in blocks
    ]
    q = [rows[0, block, at] for block in blocks]
    g = [rows[3, block, at] for block in blocks]
    scores = [dot(x, k, ((1,), (1,))) for x in q]
    masked = [jnp.where(x == columns, s, NEG_FILL) for x, s in zip(labels, scores)]
    row_max = [jnp.max(s, axis=1, keepdims=True) for s in masked]
    e = [jnp.exp2((s - m) * (SCALE * LOG2E)) for s, m in zip(masked, row_max)]
    row_total = [jnp.sum(x, axis=1, keepdims=True) for x in e]
    inverse = [jnp.where(x >= 0, 1.0 / t, 0.0) for x, t in zip(labels, row_total)]
    probs = [x * i for x, i in zip(e, inverse)]
    probs_low = [x.astype(jnp.bfloat16) for x in probs]
    attended = [dot(x, v, ((1,), (0,))) for x in probs_low]
    dprobs = [dot(x, v, ((1,), (1,))) for x in g]
    dot_term = [
        jnp.sum(x.astype(jnp.float32) * y, axis=1, keepdims=True) for x, y in zip(g, attended)
    ]
    scaled = [x * (i * SCALE) for x, i in zip(e, inverse)]
    dscore = [(x * (d - t)).astype(jnp.bfloat16) for x, d, t in zip(scaled, dprobs, dot_term)]
    query_grad = [dot(x, k, ((1,), (0,))) for x in dscore]
    for block, x, y in zip(blocks, attended, query_grad):
        results[0, block, at] = x.astype(jnp.bfloat16)
        results[1, block, at] = y.astype(jnp.bfloat16)
    key_grad = sum(dot(x, y, ((0,), (0,))) for x, y in zip(q, dscore))
    value_grad = sum(dot(x, y, ((0,), (0,))) for x, y in zip(g, probs_low))
    results[2, :, at] = key_grad.astype(jnp.bfloat16).T
    results[3, :, at] = value_grad.astype(jnp.bfloat16).T


def attend_in_loop(label_of, rows, results, key_total, value_total, head):
    at = pl.ds(pl.multiple_of(head * HD, HD), HD)
    columns = label_of(lax.broadcasted_iota(jnp.int32, (1, HALF), 1))
    k, v = rows[1, :, at], rows[2, :, at]
    key_total[...] = jnp.zeros_like(key_total)
    value_total[...] = jnp.zeros_like(value_total)

    def one(step, carry):
        start = pl.multiple_of(step * ROWS_STEP, ROWS_STEP)
        block = pl.ds(start, ROWS_STEP)
        labels = label_of(start + lax.broadcasted_iota(jnp.int32, (ROWS_STEP, 1), 0))
        q, g = rows[0, block, at], rows[3, block, at]
        masked = jnp.where(labels == columns, dot(q, k, ((1,), (1,))), NEG_FILL)
        row_max = jnp.max(masked, axis=1, keepdims=True)
        e = jnp.exp2((masked - row_max) * (SCALE * LOG2E))
        row_total = jnp.sum(e, axis=1, keepdims=True)
        inverse = jnp.where(labels >= 0, 1.0 / row_total, 0.0)
        probs = e * inverse
        probs_low = probs.astype(jnp.bfloat16)
        attended = dot(probs_low, v, ((1,), (0,)))
        dprobs = dot(g, v, ((1,), (1,)))
        dot_term = jnp.sum(g.astype(jnp.float32) * attended, axis=1, keepdims=True)
        dscore = (e * (inverse * SCALE) * (dprobs - dot_term)).astype(jnp.bfloat16)
        results[0, block, at] = attended.astype(jnp.bfloat16)
        results[1, block, at] = dot(dscore, k, ((1,), (0,))).astype(jnp.bfloat16)
        key_total[...] += dot(q, dscore, ((0,), (0,)))
        value_total[...] += dot(g, probs_low, ((0,), (0,)))
        return carry

    lax.fori_loop(0, HALF // ROWS_STEP, one, 0)
    results[2, :, at] = key_total[...].astype(jnp.bfloat16).T
    results[3, :, at] = value_total[...].astype(jnp.bfloat16).T


def gather_rows(q, k, v, g, peer, rows):
    for i, mine in enumerate((q, k, v, g)):
        rows[i, :OWN, :] = mine[...]
    rows[:, OWN:, :] = peer[...]


def near_kernel(plan, q, k, v, g, peer, out_0, out_1, out_2, out_3, peer_out, *scratch):
    rows, results, key_total, value_total = scratch
    gather_rows(q, k, v, g, peer, rows)

    def one(head, carry):
        labels = functools.partial(near_clips, plan)
        attend_in_loop(labels, rows, results, key_total, value_total, head)
        return carry

    lax.fori_loop(0, NEAR_HEADS, one, 0)
    for i, out in enumerate((out_0, out_1, out_2, out_3)):
        out[...] = results[i, :OWN, :]
    peer_out[...] = results[:, OWN:, :]


def cross_kernel(plan, q, k, v, g, peer, arrived, *rest):
    before, after, (leaving, rows, results) = rest[:5], rest[5:10], rest[10:]
    step = pl.program_id(0)
    far = plan[FAR]
    labels = functools.partial(cross_clip, plan)

    def place(frame):
        return pl.ds(pl.multiple_of(local_row(plan, plan[FARROW] + FPT * frame), FPT), FPT)

    def near_rows(start):
        row = local_row(plan, start + lax.broadcasted_iota(jnp.int32, (OWN, HD), 0))
        return (row >= plan[NEARROW]) & (row < plan[NEARROW] + FPT * plan[NEAR])

    def one(head, carry):
        at = pl.ds(pl.multiple_of(head * HD, HD), HD)
        order = (plan[PAIR] + step) * 2 + head - plan[FIRST]
        here = (order >= 0) & (order < plan[COUNT])

        def take(frame, carry):
            rows[:, place(frame), at] = arrived[order * far + frame]
            return carry

        def give(frame, carry):
            leaving[order * far + frame] = results[:, place(frame), at]
            return carry

        @pl.when(here)
        def _():
            lax.fori_loop(0, far, take, 0)
            attend(labels, rows, results, head)
            lax.fori_loop(0, far, give, 0)
            own_near, peer_near = near_rows(0), near_rows(OWN)
            for i in range(4):
                after[i][:, at] = jnp.where(own_near, results[i, :OWN, at], before[i][:, at])
                after[4][i, :, at] = jnp.where(
                    peer_near, results[i, OWN:, at], before[4][i, :, at]
                )

        @pl.when(jnp.logical_not(here))
        def _():
            for i in range(4):
                after[i][:, at] = before[i][:, at]
                after[4][i, :, at] = before[4][i, :, at]

        return carry

    @pl.when((step < plan[PAIRS]) | (step == 0))
    def _():
        gather_rows(q, k, v, g, peer, rows)
        lax.fori_loop(0, 2, one, 0)


def head_specs(heads, at):
    steps, width = MINE // heads, heads * HD
    own = [pl.BlockSpec((OWN, width), lambda i, plan: (0, plan[CORE] * steps + at(i, plan)))] * 4
    half = pl.BlockSpec((4, OWN, width), lambda i, plan: (0, 0, at(i, plan)))
    return own, half


def head_scratch(heads):
    return [pltpu.VMEM((4, HALF, heads * HD), jnp.bfloat16)] * 2


PARAMS = pltpu.CompilerParams(vmem_limit_bytes=40 * 1024 * 1024)
HALF_SHAPE = jax.ShapeDtypeStruct((4, OWN, COLS), jnp.bfloat16)
OUT_SHAPES = [jax.ShapeDtypeStruct((OWN, HEADS * HD), jnp.bfloat16)] * 4


def near_call(plan, arrays, peer):
    own, half = head_specs(NEAR_HEADS, lambda i, plan: i)
    return pl.pallas_call(
        near_kernel,
        grid_spec=pltpu.PrefetchScalarGridSpec(
            num_scalar_prefetch=1,
            grid=(MINE // NEAR_HEADS,),
            in_specs=own + [half],
            out_specs=own + [half],
            scratch_shapes=head_scratch(NEAR_HEADS) + [pltpu.VMEM((HD, HALF), jnp.float32)] * 2,
        ),
        out_shape=OUT_SHAPES + [HALF_SHAPE],
        compiler_params=PARAMS,
        name="near_clips",
    )(plan, *arrays, peer)


def cross_call(plan, arrays, peer, arrived, results):
    own, half = head_specs(
        2, lambda i, plan: plan[PAIR] + jnp.minimum(i, jnp.maximum(plan[PAIRS], 1) - 1)
    )
    whole = pl.BlockSpec(arrived.shape, lambda i, plan: (0, 0, 0, 0))
    return pl.pallas_call(
        cross_kernel,
        grid_spec=pltpu.PrefetchScalarGridSpec(
            num_scalar_prefetch=1,
            grid=(MINE // 2,),
            in_specs=own + [half, whole] + own + [half],
            out_specs=own + [half, whole],
            scratch_shapes=head_scratch(2),
        ),
        out_shape=OUT_SHAPES + [HALF_SHAPE, jax.ShapeDtypeStruct(arrived.shape, jnp.bfloat16)],
        input_output_aliases={7 + i: i for i in range(5)},
        compiler_params=PARAMS,
        name="cross_clip",
    )(plan, *arrays, peer, arrived, *results)


def near_slots(plan, body):
    near = plan[NEAR]

    def one_head(head, carry):
        def one(frame, carry):
            row = pl.multiple_of(plan[NEARROW] + FPT * frame, FPT)
            body(head * near + frame, plan[AWAY] + head, row)
            return carry

        return lax.fori_loop(0, near, one, carry)

    lax.fori_loop(0, plan[GONE], one_head, 0)


SLOTS_SHAPE = jax.ShapeDtypeStruct((SLOTS[0], 4, FPT, HD), jnp.bfloat16)


def first_kernel(place, tables, q, k, v, g, plan, mine, give):
    fill_plan(plan, place, tables)
    mine[...] = jnp.zeros_like(mine)
    give[...] = jnp.zeros_like(give)

    def body(slot, head, row):
        @pl.when((row >= OWN) == (plan[CORE] == 1))
        def _():
            at = pl.ds(pl.multiple_of(row & (OWN - 1), FPT), FPT)
            for out, core in ((mine, plan[CORE]), (give, 1 - plan[CORE])):
                col = pl.ds(pl.multiple_of((core * MINE + head) * HD, HD), HD)
                for i, x in enumerate((q, k, v, g)):
                    out[slot, i] = x[at, col]

    near_slots(plan, body)


def first_call(place, tables, arrays):
    return pl.pallas_call(
        first_kernel,
        in_specs=[SMEM] * 2 + [VMEM] * 4,
        out_specs=[SMEM, VMEM, VMEM],
        out_shape=[jax.ShapeDtypeStruct((BRANCH_IN + 1,), jnp.int32), SLOTS_SHAPE, SLOTS_SHAPE],
        compiler_params=PARAMS,
        name="first_blocks",
    )(place, tables, *arrays)


def split_kernel(place, q, k, v, g, out, sems):
    col = pl.ds(pl.multiple_of((1 - (place[1] & 1)) * COLS, COLS), COLS)
    copies = [
        pltpu.make_async_copy(x.at[:, col], out.at[i], sems.at[i])
        for i, x in enumerate((q, k, v, g))
    ]
    for c in copies:
        c.start()
    for c in copies:
        c.wait()


def split_call(place, arrays):
    return pl.pallas_call(
        split_kernel,
        in_specs=[SMEM] + [ANY] * 4,
        out_specs=VMEM,
        out_shape=HALF_SHAPE,
        scratch_shapes=[pltpu.SemaphoreType.DMA((4,))],
        compiler_params=PARAMS,
        name="split_heads",
    )(place, *arrays)


def join_kernel(plan, other, *rest):
    for i, out in enumerate(rest[4:]):
        out[...] = other[i]


def join_call(plan, other, outs):
    width = COLS // JOIN_STEPS
    block = pl.BlockSpec((OWN, width), lambda i, plan: (0, (1 - plan[CORE]) * JOIN_STEPS + i))
    return pl.pallas_call(
        join_kernel,
        grid_spec=pltpu.PrefetchScalarGridSpec(
            num_scalar_prefetch=1,
            grid=(JOIN_STEPS,),
            in_specs=[pl.BlockSpec((4, OWN, width), lambda i, plan: (0, 0, i))] + [ANY] * 4,
            out_specs=[block] * 4,
        ),
        out_shape=OUT_SHAPES,
        input_output_aliases={2 + i: i for i in range(4)},
        compiler_params=PARAMS,
        name="join_halves",
    )(plan, other, *outs)


def unpack_kernel(plan, mine, other, *rest):
    outs, sems = rest[4:8], rest[8]

    def each(act):
        def body(slot, head, row):
            @pl.when((row >= OWN) == (plan[CORE] == 1))
            def _():
                at = pl.ds(pl.multiple_of(row & (OWN - 1), FPT), FPT)
                for j, back in enumerate((mine, other)):
                    core = plan[CORE] if j == 0 else 1 - plan[CORE]
                    col = pl.ds(pl.multiple_of((core * MINE + head) * HD, HD), HD)
                    for i, out in enumerate(outs):
                        act(
                            pltpu.make_async_copy(
                                back.at[slot, i], out.at[at, col], sems.at[slot, j, i]
                            )
                        )

        near_slots(plan, body)

    each(lambda c: c.start())
    each(lambda c: c.wait())


def unpack_call(plan, mine, other, outs):
    return pl.pallas_call(
        unpack_kernel,
        in_specs=[SMEM, VMEM, VMEM] + [ANY] * 4,
        out_specs=[ANY] * 4,
        out_shape=OUT_SHAPES,
        input_output_aliases={3: 0, 4: 1, 5: 2, 6: 3},
        scratch_shapes=[pltpu.SemaphoreType.DMA((mine.shape[0], 2, 4))],
        compiler_params=PARAMS,
        name="unpack_cross",
    )(plan, mine, other, *outs)


OTHER_CORE = [(i, i ^ 1) for i in range(4)]
OTHER_CHIP = [(i, i ^ 2) for i in range(4)]


def branch_in(slots, late=False):
    def run(plan, arrays, peer, mine, got):
        if not slots:
            return near_call(plan, arrays, peer), jnp.zeros(SLOTS_SHAPE.shape, jnp.bfloat16)
        leaving = mine[:slots] + got[:slots]
        if late:
            results = near_call(plan, arrays, peer)
            leaving, results = lax.optimization_barrier((leaving, results))
        arrived = lax.ppermute(leaving, "ulysses", OTHER_CHIP)
        if not late:
            results = near_call(plan, arrays, peer)
            results, arrived = lax.optimization_barrier((results, arrived))
        return results, pad_slots(arrived)

    return run


def branch_out(slots):
    def run(plan, results, leaving):
        if slots:
            returned = lax.ppermute(leaving[:slots], "ulysses", OTHER_CHIP)
        other = lax.ppermute(results[4], "ulysses", OTHER_CORE)
        outs = join_call(plan, other, results[:4])
        if not slots:
            return outs, jnp.zeros(SLOTS_SHAPE.shape, jnp.bfloat16)
        outs, returned = lax.optimization_barrier((outs, returned))
        return outs, pad_slots(returned)

    return run


def pad_slots(blocks):
    return jnp.pad(blocks, ((0, SLOTS[0] - blocks.shape[0]), (0, 0), (0, 0), (0, 0)))


def shards(queries, key_rows, values, out_grad, frames, offsets):
    place = jnp.stack([lax.axis_index("dp"), lax.axis_index("ulysses")]).astype(jnp.int32)
    arrays = (queries, key_rows, values, out_grad)
    sent = split_call(place, arrays)
    peer = lax.ppermute(sent, "ulysses", OTHER_CORE)
    tables = jnp.concatenate([frames.T, offsets.T])
    sent, tables, place = lax.optimization_barrier((sent, tables, place))
    plan, mine, give = first_call(place, tables, arrays)
    got = lax.ppermute(give, "ulysses", OTHER_CORE)
    ways_in = [branch_in(n) for n in SLOTS] + [branch_in(n, late=True) for n in LATE_SLOTS]
    results, arrived = lax.switch(plan[BRANCH_IN], ways_in, plan, arrays, peer, mine, got)
    *results, leaving = cross_call(plan, arrays, peer, arrived, results)
    outs, returned = lax.switch(
        plan[BRANCH], [branch_out(n) for n in SLOTS], plan, results, leaving
    )
    returned_other = lax.ppermute(returned, "ulysses", OTHER_CORE)
    return tuple(unpack_call(plan, returned, returned_other, outs))


def solution(mesh):
    rows = P(("dp", "ulysses"), None)
    return jax.shard_map(
        shards,
        mesh=mesh,
        in_specs=(rows, rows, rows, rows, P(), P()),
        out_specs=(rows, rows, rows, rows),
        check_vma=False,
    )
```

```python
import functools
import math

import jax
import jax.numpy as jnp
from jax import lax
from jax.experimental import pallas as pl
from jax.experimental.pallas import tpu as pltpu
from jax.sharding import PartitionSpec as P

HEADS = 20
HD = 128
FPT = 64
FPT_BITS = 6
HALF = 512
OWN = 256
MINE = 10
COLS = MINE * HD
NEG_FILL = -1e30
ANY = pl.BlockSpec(memory_space=pl.ANY)
SMEM = pl.BlockSpec(memory_space=pltpu.SMEM)
VMEM = pl.BlockSpec(memory_space=pltpu.VMEM)
SCALE = 1.0 / math.sqrt(HD)
LOG2E = math.log2(math.e)
ROWS_STEP = 256
JOIN_STEPS = 5
NEAR_HEADS = 2

SLOTS = (20, 18, 15, 12, 10, 0)
LATE_SLOTS = (20, 15, 10)


CORE, B0, E0, B1, E1, PA, PB, FIRST, COUNT, NEAR, FAR, NEARROW, FARROW, AWAY, GONE, PAIR, PAIRS, BRANCH, BRANCH_IN = range(19)


def split_heads(a, b):
    best, heads = jnp.maximum(a, b * (MINE - 1)), 1
    for h in range(2, MINE):
        cost = jnp.maximum(a * h, b * (MINE - h))
        heads = jnp.where(cost < best, h, heads)
        best = jnp.minimum(cost, best)
    return heads, jnp.where((a > 0) & (b > 0), best, 0)


def crossing(tables, group):
    a = b = 0
    for i in range(2):
        begin = tables[2 + i, group]
        end = begin + tables[i, group] * FPT
        crosses = (begin < HALF) & (end > HALF)
        a = jnp.where(crosses, (HALF - begin) >> FPT_BITS, a)
        b = jnp.where(crosses, (end - HALF) >> FPT_BITS, b)
    return (a, b, *split_heads(a, b))


def place_in(choices, cost):
    found = 0
    for i, n in enumerate(choices[1:]):
        found = jnp.where(cost <= n, i + 1, found)
    return found


def fill_plan(plan, place, tables):
    group, core, high = place[0], place[1] & 1, place[1] >> 1
    base = high * HALF
    for i, (begin_at, end_at) in enumerate(((B0, E0), (B1, E1))):
        begin = tables[2 + i, group]
        end = begin + tables[i, group] * FPT
        crosses = (begin < HALF) & (end > HALF)
        plan[begin_at] = jnp.where(crosses, 0, begin - base)
        plan[end_at] = jnp.where(crosses, 0, end - base)
    a, b, h, cost = crossing(tables, group)
    other = crossing(tables, group ^ 2)[3]
    late = (cost > 0) & ((other > cost) | ((other == cost) & ((group & 2) == 2)))
    branch = place_in(SLOTS, cost)
    plan[BRANCH_IN] = jnp.where(late, len(SLOTS) + place_in(LATE_SLOTS, cost), branch)
    second = high == 1
    plan[CORE] = core
    plan[PA] = FPT * a
    plan[PB] = FPT * b
    plan[FIRST] = jnp.where(second, 0, h)
    plan[COUNT] = jnp.where(cost == 0, 0, jnp.where(second, h, MINE - h))
    plan[GONE] = jnp.where(cost == 0, 0, jnp.where(second, MINE - h, h))
    plan[NEAR] = jnp.where(second, b, a)
    plan[FAR] = jnp.where(second, a, b)
    plan[NEARROW] = jnp.where(second, 0, HALF - FPT * a)
    plan[FARROW] = jnp.where(second, HALF - FPT * a, 0)
    plan[PAIR] = jnp.where(second, 0, h >> 1)
    plan[PAIRS] = jnp.where(cost == 0, 0, jnp.where(second, (h + 1) >> 1, MINE // 2 - (h >> 1)))
    plan[AWAY] = jnp.where(second, h, 0)
    plan[BRANCH] = branch


def local_row(plan, position):
    return (position + OWN * plan[CORE]) & (HALF - 1)


def near_clips(plan, position):
    row = local_row(plan, position)
    first = (row >= plan[B0]) & (row < plan[E0])
    second = (row >= plan[B1]) & (row < plan[E1])
    return jnp.where(first, 0, jnp.where(second, 1, -1))


def cross_clip(plan, position):
    row = local_row(plan, position)
    return jnp.where((row < plan[PB]) | (row >= HALF - plan[PA]), 0, -1)


def dot(x, y, dims):
    return lax.dot_general(x, y, (dims, ((), ())), preferred_element_type=jnp.float32)


def attend(label_of, rows, results, head):
    at = pl.ds(pl.multiple_of(head * HD, HD), HD)
    columns = label_of(lax.broadcasted_iota(jnp.int32, (1, HALF), 1))
    k, v = rows[1, :, at], rows[2, :, at]
    blocks = [pl.ds(start, ROWS_STEP) for start in range(0, HALF, ROWS_STEP)]
    labels = [
        label_of(block.start + lax.broadcasted_iota(jnp.int32, (ROWS_STEP, 1), 0))
        for block in blocks
    ]
    q = [rows[0, block, at] for block in blocks]
    g = [rows[3, block, at] for block in blocks]
    scores = [dot(x, k, ((1,), (1,))) for x in q]
    masked = [jnp.where(x == columns, s, NEG_FILL) for x, s in zip(labels, scores)]
    row_max = [jnp.max(s, axis=1, keepdims=True) for s in masked]
    e = [jnp.exp2((s - m) * (SCALE * LOG2E)) for s, m in zip(masked, row_max)]
    row_total = [jnp.sum(x, axis=1, keepdims=True) for x in e]
    inverse = [jnp.where(x >= 0, 1.0 / t, 0.0) for x, t in zip(labels, row_total)]
    probs = [x * i for x, i in zip(e, inverse)]
    probs_low = [x.astype(jnp.bfloat16) for x in probs]
    attended = [dot(x, v, ((1,), (0,))) for x in probs_low]
    dprobs = [dot(x, v, ((1,), (1,))) for x in g]
    dot_term = [
        jnp.sum(x.astype(jnp.float32) * y, axis=1, keepdims=True) for x, y in zip(g, attended)
    ]
    scaled = [x * (i * SCALE) for x, i in zip(e, inverse)]
    dscore = [(x * (d - t)).astype(jnp.bfloat16) for x, d, t in zip(scaled, dprobs, dot_term)]
    query_grad = [dot(x, k, ((1,), (0,))) for x in dscore]
    for block, x, y in zip(blocks, attended, query_grad):
        results[0, block, at] = x.astype(jnp.bfloat16)
        results[1, block, at] = y.astype(jnp.bfloat16)
    key_grad = sum(dot(x, y, ((0,), (0,))) for x, y in zip(q, dscore))
    value_grad = sum(dot(x, y, ((0,), (0,))) for x, y in zip(g, probs_low))
    results[2, :, at] = key_grad.astype(jnp.bfloat16).T
    results[3, :, at] = value_grad.astype(jnp.bfloat16).T


def attend_in_loop(label_of, rows, results, key_total, value_total, head):
    at = pl.ds(pl.multiple_of(head * HD, HD), HD)
    columns = label_of(lax.broadcasted_iota(jnp.int32, (1, HALF), 1))
    k, v = rows[1, :, at], rows[2, :, at]
    key_total[...] = jnp.zeros_like(key_total)
    value_total[...] = jnp.zeros_like(value_total)

    def one(step, carry):
        start = pl.multiple_of(step * ROWS_STEP, ROWS_STEP)
        block = pl.ds(start, ROWS_STEP)
        labels = label_of(start + lax.broadcasted_iota(jnp.int32, (ROWS_STEP, 1), 0))
        q, g = rows[0, block, at], rows[3, block, at]
        masked = jnp.where(labels == columns, dot(q, k, ((1,), (1,))), NEG_FILL)
        row_max = jnp.max(masked, axis=1, keepdims=True)
        e = jnp.exp2((masked - row_max) * (SCALE * LOG2E))
        row_total = jnp.sum(e, axis=1, keepdims=True)
        inverse = jnp.where(labels >= 0, 1.0 / row_total, 0.0)
        probs = e * inverse
        probs_low = probs.astype(jnp.bfloat16)
        attended = dot(probs_low, v, ((1,), (0,)))
        dprobs = dot(g, v, ((1,), (1,)))
        dot_term = jnp.sum(g.astype(jnp.float32) * attended, axis=1, keepdims=True)
        dscore = (e * (inverse * SCALE) * (dprobs - dot_term)).astype(jnp.bfloat16)
        results[0, block, at] = attended.astype(jnp.bfloat16)
        results[1, block, at] = dot(dscore, k, ((1,), (0,))).astype(jnp.bfloat16)
        key_total[...] += dot(q, dscore, ((0,), (0,)))
        value_total[...] += dot(g, probs_low, ((0,), (0,)))
        return carry

    lax.fori_loop(0, HALF // ROWS_STEP, one, 0)
    results[2, :, at] = key_total[...].astype(jnp.bfloat16).T
    results[3, :, at] = value_total[...].astype(jnp.bfloat16).T


def gather_rows(q, k, v, g, peer, rows):
    for i, mine in enumerate((q, k, v, g)):
        rows[i, :OWN, :] = mine[...]
    rows[:, OWN:, :] = peer[...]


def near_kernel(plan, q, k, v, g, peer, out_0, out_1, out_2, out_3, peer_out, *scratch):
    rows, results, key_total, value_total = scratch
    gather_rows(q, k, v, g, peer, rows)

    def one(head, carry):
        labels = functools.partial(near_clips, plan)
        attend_in_loop(labels, rows, results, key_total, value_total, head)
        return carry

    lax.fori_loop(0, NEAR_HEADS, one, 0)
    for i, out in enumerate((out_0, out_1, out_2, out_3)):
        out[...] = results[i, :OWN, :]
    peer_out[...] = results[:, OWN:, :]


def cross_kernel(plan, q, k, v, g, peer, arrived, *rest):
    before, after, (leaving, rows, results) = rest[:5], rest[5:10], rest[10:]
    step = pl.program_id(0)
    far = plan[FAR]
    labels = functools.partial(cross_clip, plan)

    def place(frame):
        return pl.ds(pl.multiple_of(local_row(plan, plan[FARROW] + FPT * frame), FPT), FPT)

    def near_rows(start):
        row = local_row(plan, start + lax.broadcasted_iota(jnp.int32, (OWN, HD), 0))
        return (row >= plan[NEARROW]) & (row < plan[NEARROW] + FPT * plan[NEAR])

    def one(head, carry):
        at = pl.ds(pl.multiple_of(head * HD, HD), HD)
        order = (plan[PAIR] + step) * 2 + head - plan[FIRST]
        here = (order >= 0) & (order < plan[COUNT])

        def take(frame, carry):
            rows[:, place(frame), at] = arrived[order * far + frame]
            return carry

        def give(frame, carry):
            leaving[order * far + frame] = results[:, place(frame), at]
            return carry

        @pl.when(here)
        def _():
            lax.fori_loop(0, far, take, 0)
            attend(labels, rows, results, head)
            lax.fori_loop(0, far, give, 0)
            own_near, peer_near = near_rows(0), near_rows(OWN)
            for i in range(4):
                after[i][:, at] = jnp.where(own_near, results[i, :OWN, at], before[i][:, at])
                after[4][i, :, at] = jnp.where(
                    peer_near, results[i, OWN:, at], before[4][i, :, at]
                )

        @pl.when(jnp.logical_not(here))
        def _():
            for i in range(4):
                after[i][:, at] = before[i][:, at]
                after[4][i, :, at] = before[4][i, :, at]

        return carry

    @pl.when((step < plan[PAIRS]) | (step == 0))
    def _():
        gather_rows(q, k, v, g, peer, rows)
        lax.fori_loop(0, 2, one, 0)


def head_specs(heads, at):
    steps, width = MINE // heads, heads * HD
    own = [pl.BlockSpec((OWN, width), lambda i, plan: (0, plan[CORE] * steps + at(i, plan)))] * 4
    half = pl.BlockSpec((4, OWN, width), lambda i, plan: (0, 0, at(i, plan)))
    return own, half


def head_scratch(heads):
    return [pltpu.VMEM((4, HALF, heads * HD), jnp.bfloat16)] * 2


PARAMS = pltpu.CompilerParams(vmem_limit_bytes=40 * 1024 * 1024)
HALF_SHAPE = jax.ShapeDtypeStruct((4, OWN, COLS), jnp.bfloat16)
OUT_SHAPES = [jax.ShapeDtypeStruct((OWN, HEADS * HD), jnp.bfloat16)] * 4


def near_call(plan, arrays, peer):
    own, half = head_specs(NEAR_HEADS, lambda i, plan: i)
    return pl.pallas_call(
        near_kernel,
        grid_spec=pltpu.PrefetchScalarGridSpec(
            num_scalar_prefetch=1,
            grid=(MINE // NEAR_HEADS,),
            in_specs=own + [half],
            out_specs=own + [half],
            scratch_shapes=head_scratch(NEAR_HEADS) + [pltpu.VMEM((HD, HALF), jnp.float32)] * 2,
        ),
        out_shape=OUT_SHAPES + [HALF_SHAPE],
        compiler_params=PARAMS,
        name="near_clips",
    )(plan, *arrays, peer)


def cross_call(plan, arrays, peer, arrived, results):
    own, half = head_specs(
        2, lambda i, plan: plan[PAIR] + jnp.minimum(i, jnp.maximum(plan[PAIRS], 1) - 1)
    )
    whole = pl.BlockSpec(arrived.shape, lambda i, plan: (0, 0, 0, 0))
    return pl.pallas_call(
        cross_kernel,
        grid_spec=pltpu.PrefetchScalarGridSpec(
            num_scalar_prefetch=1,
            grid=(MINE // 2,),
            in_specs=own + [half, whole] + own + [half],
            out_specs=own + [half, whole],
            scratch_shapes=head_scratch(2),
        ),
        out_shape=OUT_SHAPES + [HALF_SHAPE, jax.ShapeDtypeStruct(arrived.shape, jnp.bfloat16)],
        input_output_aliases={7 + i: i for i in range(5)},
        compiler_params=PARAMS,
        name="cross_clip",
    )(plan, *arrays, peer, arrived, *results)


def near_slots(plan, body):
    near = plan[NEAR]

    def one_head(head, carry):
        def one(frame, carry):
            row = pl.multiple_of(plan[NEARROW] + FPT * frame, FPT)
            body(head * near + frame, plan[AWAY] + head, row)
            return carry

        return lax.fori_loop(0, near, one, carry)

    lax.fori_loop(0, plan[GONE], one_head, 0)


SLOTS_SHAPE = jax.ShapeDtypeStruct((SLOTS[0], 4, FPT, HD), jnp.bfloat16)


def first_kernel(place, tables, q, k, v, g, plan, mine, give):
    fill_plan(plan, place, tables)
    mine[...] = jnp.zeros_like(mine)
    give[...] = jnp.zeros_like(give)

    def body(slot, head, row):
        @pl.when((row >= OWN) == (plan[CORE] == 1))
        def _():
            at = pl.ds(pl.multiple_of(row & (OWN - 1), FPT), FPT)
            for out, core in ((mine, plan[CORE]), (give, 1 - plan[CORE])):
                col = pl.ds(pl.multiple_of((core * MINE + head) * HD, HD), HD)
                for i, x in enumerate((q, k, v, g)):
                    out[slot, i] = x[at, col]

    near_slots(plan, body)


def first_call(place, tables, arrays):
    return pl.pallas_call(
        first_kernel,
        in_specs=[SMEM] * 2 + [VMEM] * 4,
        out_specs=[SMEM, VMEM, VMEM],
        out_shape=[jax.ShapeDtypeStruct((BRANCH_IN + 1,), jnp.int32), SLOTS_SHAPE, SLOTS_SHAPE],
        compiler_params=PARAMS,
        name="first_blocks",
    )(place, tables, *arrays)


def split_kernel(place, q, k, v, g, out, sems):
    col = pl.ds(pl.multiple_of((1 - (place[1] & 1)) * COLS, COLS), COLS)
    copies = [
        pltpu.make_async_copy(x.at[:, col], out.at[i], sems.at[i])
        for i, x in enumerate((q, k, v, g))
    ]
    for c in copies:
        c.start()
    for c in copies:
        c.wait()


def split_call(place, arrays):
    return pl.pallas_call(
        split_kernel,
        in_specs=[SMEM] + [ANY] * 4,
        out_specs=VMEM,
        out_shape=HALF_SHAPE,
        scratch_shapes=[pltpu.SemaphoreType.DMA((4,))],
        compiler_params=PARAMS,
        name="split_heads",
    )(place, *arrays)


def join_kernel(plan, other, *rest):
    for i, out in enumerate(rest[4:]):
        out[...] = other[i]


def join_call(plan, other, outs):
    width = COLS // JOIN_STEPS
    block = pl.BlockSpec((OWN, width), lambda i, plan: (0, (1 - plan[CORE]) * JOIN_STEPS + i))
    return pl.pallas_call(
        join_kernel,
        grid_spec=pltpu.PrefetchScalarGridSpec(
            num_scalar_prefetch=1,
            grid=(JOIN_STEPS,),
            in_specs=[pl.BlockSpec((4, OWN, width), lambda i, plan: (0, 0, i))] + [ANY] * 4,
            out_specs=[block] * 4,
        ),
        out_shape=OUT_SHAPES,
        input_output_aliases={2 + i: i for i in range(4)},
        compiler_params=PARAMS,
        name="join_halves",
    )(plan, other, *outs)


def unpack_kernel(plan, mine, other, *rest):
    outs, sems = rest[4:8], rest[8]

    def each(act):
        def body(slot, head, row):
            @pl.when((row >= OWN) == (plan[CORE] == 1))
            def _():
                at = pl.ds(pl.multiple_of(row & (OWN - 1), FPT), FPT)
                for j, back in enumerate((mine, other)):
                    core = plan[CORE] if j == 0 else 1 - plan[CORE]
                    col = pl.ds(pl.multiple_of((core * MINE + head) * HD, HD), HD)
                    for i, out in enumerate(outs):
                        act(
                            pltpu.make_async_copy(
                                back.at[slot, i], out.at[at, col], sems.at[slot, j, i]
                            )
                        )

        near_slots(plan, body)

    each(lambda c: c.start())
    each(lambda c: c.wait())


def unpack_call(plan, mine, other, outs):
    return pl.pallas_call(
        unpack_kernel,
        in_specs=[SMEM, VMEM, VMEM] + [ANY] * 4,
        out_specs=[ANY] * 4,
        out_shape=OUT_SHAPES,
        input_output_aliases={3: 0, 4: 1, 5: 2, 6: 3},
        scratch_shapes=[pltpu.SemaphoreType.DMA((mine.shape[0], 2, 4))],
        compiler_params=PARAMS,
        name="unpack_cross",
    )(plan, mine, other, *outs)


OTHER_CORE = [(i, i ^ 1) for i in range(4)]
OTHER_CHIP = [(i, i ^ 2) for i in range(4)]


def branch_in(slots, late=False):
    def run(plan, arrays, peer, mine, got):
        if not slots:
            return near_call(plan, arrays, peer), jnp.zeros(SLOTS_SHAPE.shape, jnp.bfloat16)
        leaving = mine[:slots] + got[:slots]
        if late:
            results = near_call(plan, arrays, peer)
            leaving, results = lax.optimization_barrier((leaving, results))
        arrived = lax.ppermute(leaving, "ulysses", OTHER_CHIP)
        if not late:
            results = near_call(plan, arrays, peer)
            results, arrived = lax.optimization_barrier((results, arrived))
        return results, pad_slots(arrived)

    return run


def branch_out(slots):
    def run(plan, results, leaving):
        if slots:
            returned = lax.ppermute(leaving[:slots], "ulysses", OTHER_CHIP)
        other = lax.ppermute(results[4], "ulysses", OTHER_CORE)
        outs = join_call(plan, other, results[:4])
        if not slots:
            return outs, jnp.zeros(SLOTS_SHAPE.shape, jnp.bfloat16)
        outs, returned = lax.optimization_barrier((outs, returned))
        return outs, pad_slots(returned)

    return run


def pad_slots(blocks):
    return jnp.pad(blocks, ((0, SLOTS[0] - blocks.shape[0]), (0, 0), (0, 0), (0, 0)))


def shards(queries, key_rows, values, out_grad, frames, offsets):
    place = jnp.stack([lax.axis_index("dp"), lax.axis_index("ulysses")]).astype(jnp.int32)
    arrays = (queries, key_rows, values, out_grad)
    sent = split_call(place, arrays)
    peer = lax.ppermute(sent, "ulysses", OTHER_CORE)
    tables = jnp.concatenate([frames.T, offsets.T])
    sent, tables, place = lax.optimization_barrier((sent, tables, place))
    plan, mine, give = first_call(place, tables, arrays)
    got = lax.ppermute(give, "ulysses", OTHER_CORE)
    ways_in = [branch_in(n) for n in SLOTS] + [branch_in(n, late=True) for n in LATE_SLOTS]
    results, arrived = lax.switch(plan[BRANCH_IN], ways_in, plan, arrays, peer, mine, got)
    *results, leaving = cross_call(plan, arrays, peer, arrived, results)
    outs, returned = lax.switch(
        plan[BRANCH], [branch_out(n) for n in SLOTS], plan, results, leaving
    )
    returned_other = lax.ppermute(returned, "ulysses", OTHER_CORE)
    return tuple(unpack_call(plan, returned, returned_other, outs))


def solution(mesh):
    rows = P(("dp", "ulysses"), None)
    return jax.shard_map(
        shards,
        mesh=mesh,
        in_specs=(rows, rows, rows, rows, P(), P()),
        out_specs=(rows, rows, rows, rows),
        check_vma=False,
    )
```

```python
import functools
import math

import jax
import jax.numpy as jnp
from jax import lax
from jax.experimental import pallas as pl
from jax.experimental.pallas import tpu as pltpu
from jax.sharding import PartitionSpec as P

HEADS = 20
HD = 128
FPT = 64
FPT_BITS = 6
HALF = 512
OWN = 256
MINE = 10
COLS = MINE * HD
NEG_FILL = -1e30
ANY = pl.BlockSpec(memory_space=pl.ANY)
SMEM = pl.BlockSpec(memory_space=pltpu.SMEM)
VMEM = pl.BlockSpec(memory_space=pltpu.VMEM)
SCALE = 1.0 / math.sqrt(HD)
LOG2E = math.log2(math.e)
ROWS_STEP = 256
JOIN_STEPS = 5
NEAR_HEADS = 2

SLOTS = (20, 18, 15, 12, 10, 0)
LATE_SLOTS = (20, 15, 10)


CORE, B0, E0, B1, E1, PA, PB, FIRST, COUNT, NEAR, FAR, NEARROW, FARROW, AWAY, GONE, PAIR, PAIRS, BRANCH, BRANCH_IN = range(19)


def split_heads(a, b):
    best, heads = jnp.maximum(a, b * (MINE - 1)), 1
    for h in range(2, MINE):
        cost = jnp.maximum(a * h, b * (MINE - h))
        heads = jnp.where(cost < best, h, heads)
        best = jnp.minimum(cost, best)
    return heads, jnp.where((a > 0) & (b > 0), best, 0)


def crossing(tables, group):
    a = b = 0
    for i in range(2):
        begin = tables[2 + i, group]
        end = begin + tables[i, group] * FPT
        crosses = (begin < HALF) & (end > HALF)
        a = jnp.where(crosses, (HALF - begin) >> FPT_BITS, a)
        b = jnp.where(crosses, (end - HALF) >> FPT_BITS, b)
    return (a, b, *split_heads(a, b))


def place_in(choices, cost):
    found = 0
    for i, n in enumerate(choices[1:]):
        found = jnp.where(cost <= n, i + 1, found)
    return found


def fill_plan(plan, place, tables):
    group, core, high = place[0], place[1] & 1, place[1] >> 1
    base = high * HALF
    for i, (begin_at, end_at) in enumerate(((B0, E0), (B1, E1))):
        begin = tables[2 + i, group]
        end = begin + tables[i, group] * FPT
        crosses = (begin < HALF) & (end > HALF)
        plan[begin_at] = jnp.where(crosses, 0, begin - base)
        plan[end_at] = jnp.where(crosses, 0, end - base)
    a, b, h, cost = crossing(tables, group)
    other = crossing(tables, group ^ 2)[3]
    late = (cost > 0) & ((other > cost) | ((other == cost) & ((group & 2) == 2)))
    branch = place_in(SLOTS, cost)
    plan[BRANCH_IN] = jnp.where(late, len(SLOTS) + place_in(LATE_SLOTS, cost), branch)
    second = high == 1
    plan[CORE] = core
    plan[PA] = FPT * a
    plan[PB] = FPT * b
    plan[FIRST] = jnp.where(second, 0, h)
    plan[COUNT] = jnp.where(cost == 0, 0, jnp.where(second, h, MINE - h))
    plan[GONE] = jnp.where(cost == 0, 0, jnp.where(second, MINE - h, h))
    plan[NEAR] = jnp.where(second, b, a)
    plan[FAR] = jnp.where(second, a, b)
    plan[NEARROW] = jnp.where(second, 0, HALF - FPT * a)
    plan[FARROW] = jnp.where(second, HALF - FPT * a, 0)
    plan[PAIR] = jnp.where(second, 0, h >> 1)
    plan[PAIRS] = jnp.where(cost == 0, 0, jnp.where(second, (h + 1) >> 1, MINE // 2 - (h >> 1)))
    plan[AWAY] = jnp.where(second, h, 0)
    plan[BRANCH] = branch


def local_row(plan, position):
    return (position + OWN * plan[CORE]) & (HALF - 1)


def near_clips(plan, position):
    row = local_row(plan, position)
    first = (row >= plan[B0]) & (row < plan[E0])
    second = (row >= plan[B1]) & (row < plan[E1])
    return jnp.where(first, 0, jnp.where(second, 1, -1))


def cross_clip(plan, position):
    row = local_row(plan, position)
    return jnp.where((row < plan[PB]) | (row >= HALF - plan[PA]), 0, -1)


def dot(x, y, dims):
    return lax.dot_general(x, y, (dims, ((), ())), preferred_element_type=jnp.float32)


def attend(label_of, rows, results, head):
    at = pl.ds(pl.multiple_of(head * HD, HD), HD)
    columns = label_of(lax.broadcasted_iota(jnp.int32, (1, HALF), 1))
    k, v = rows[1, :, at], rows[2, :, at]
    blocks = [pl.ds(start, ROWS_STEP) for start in range(0, HALF, ROWS_STEP)]
    labels = [
        label_of(block.start + lax.broadcasted_iota(jnp.int32, (ROWS_STEP, 1), 0))
        for block in blocks
    ]
    q = [rows[0, block, at] for block in blocks]
    g = [rows[3, block, at] for block in blocks]
    scores = [dot(x, k, ((1,), (1,))) for x in q]
    masked = [jnp.where(x == columns, s, NEG_FILL) for x, s in zip(labels, scores)]
    row_max = [jnp.max(s, axis=1, keepdims=True) for s in masked]
    e = [jnp.exp2((s - m) * (SCALE * LOG2E)) for s, m in zip(masked, row_max)]
    row_total = [jnp.sum(x, axis=1, keepdims=True) for x in e]
    inverse = [jnp.where(x >= 0, 1.0 / t, 0.0) for x, t in zip(labels, row_total)]
    probs = [x * i for x, i in zip(e, inverse)]
    probs_low = [x.astype(jnp.bfloat16) for x in probs]
    attended = [dot(x, v, ((1,), (0,))) for x in probs_low]
    dprobs = [dot(x, v, ((1,), (1,))) for x in g]
    dot_term = [
        jnp.sum(x.astype(jnp.float32) * y, axis=1, keepdims=True) for x, y in zip(g, attended)
    ]
    scaled = [x * (i * SCALE) for x, i in zip(e, inverse)]
    dscore = [(x * (d - t)).astype(jnp.bfloat16) for x, d, t in zip(scaled, dprobs, dot_term)]
    query_grad = [dot(x, k, ((1,), (0,))) for x in dscore]
    for block, x, y in zip(blocks, attended, query_grad):
        results[0, block, at] = x.astype(jnp.bfloat16)
        results[1, block, at] = y.astype(jnp.bfloat16)
    key_grad = sum(dot(x, y, ((0,), (0,))) for x, y in zip(q, dscore))
    value_grad = sum(dot(x, y, ((0,), (0,))) for x, y in zip(g, probs_low))
    results[2, :, at] = key_grad.astype(jnp.bfloat16).T
    results[3, :, at] = value_grad.astype(jnp.bfloat16).T


def attend_in_loop(label_of, rows, results, key_total, value_total, head):
    at = pl.ds(pl.multiple_of(head * HD, HD), HD)
    columns = label_of(lax.broadcasted_iota(jnp.int32, (1, HALF), 1))
    k, v = rows[1, :, at], rows[2, :, at]
    key_total[...] = jnp.zeros_like(key_total)
    value_total[...] = jnp.zeros_like(value_total)

    def one(step, carry):
        start = pl.multiple_of(step * ROWS_STEP, ROWS_STEP)
        block = pl.ds(start, ROWS_STEP)
        labels = label_of(start + lax.broadcasted_iota(jnp.int32, (ROWS_STEP, 1), 0))
        q, g = rows[0, block, at], rows[3, block, at]
        masked = jnp.where(labels == columns, dot(q, k, ((1,), (1,))), NEG_FILL)
        row_max = jnp.max(masked, axis=1, keepdims=True)
        e = jnp.exp2((masked - row_max) * (SCALE * LOG2E))
        row_total = jnp.sum(e, axis=1, keepdims=True)
        inverse = jnp.where(labels >= 0, 1.0 / row_total, 0.0)
        probs = e * inverse
        probs_low = probs.astype(jnp.bfloat16)
        attended = dot(probs_low, v, ((1,), (0,)))
        dprobs = dot(g, v, ((1,), (1,)))
        dot_term = jnp.sum(g.astype(jnp.float32) * attended, axis=1, keepdims=True)
        dscore = (e * (inverse * SCALE) * (dprobs - dot_term)).astype(jnp.bfloat16)
        results[0, block, at] = attended.astype(jnp.bfloat16)
        results[1, block, at] = dot(dscore, k, ((1,), (0,))).astype(jnp.bfloat16)
        key_total[...] += dot(q, dscore, ((0,), (0,)))
        value_total[...] += dot(g, probs_low, ((0,), (0,)))
        return carry

    lax.fori_loop(0, HALF // ROWS_STEP, one, 0)
    results[2, :, at] = key_total[...].astype(jnp.bfloat16).T
    results[3, :, at] = value_total[...].astype(jnp.bfloat16).T


def gather_rows(q, k, v, g, peer, rows):
    for i, mine in enumerate((q, k, v, g)):
        rows[i, :OWN, :] = mine[...]
    rows[:, OWN:, :] = peer[...]


def near_kernel(plan, q, k, v, g, peer, out_0, out_1, out_2, out_3, peer_out, *scratch):
    rows, results, key_total, value_total = scratch
    gather_rows(q, k, v, g, peer, rows)

    def one(head, carry):
        labels = functools.partial(near_clips, plan)
        attend_in_loop(labels, rows, results, key_total, value_total, head)
        return carry

    lax.fori_loop(0, NEAR_HEADS, one, 0)
    for i, out in enumerate((out_0, out_1, out_2, out_3)):
        out[...] = results[i, :OWN, :]
    peer_out[...] = results[:, OWN:, :]


def cross_kernel(plan, q, k, v, g, peer, arrived, *rest):
    before, after, (leaving, rows, results) = rest[:5], rest[5:10], rest[10:]
    step = pl.program_id(0)
    far = plan[FAR]
    labels = functools.partial(cross_clip, plan)

    def place(frame):
        return pl.ds(pl.multiple_of(local_row(plan, plan[FARROW] + FPT * frame), FPT), FPT)

    def near_rows(start):
        row = local_row(plan, start + lax.broadcasted_iota(jnp.int32, (OWN, HD), 0))
        return (row >= plan[NEARROW]) & (row < plan[NEARROW] + FPT * plan[NEAR])

    def one(head, carry):
        at = pl.ds(pl.multiple_of(head * HD, HD), HD)
        order = (plan[PAIR] + step) * 2 + head - plan[FIRST]
        here = (order >= 0) & (order < plan[COUNT])

        def take(frame, carry):
            rows[:, place(frame), at] = arrived[order * far + frame]
            return carry

        def give(frame, carry):
            leaving[order * far + frame] = results[:, place(frame), at]
            return carry

        @pl.when(here)
        def _():
            lax.fori_loop(0, far, take, 0)
            attend(labels, rows, results, head)
            lax.fori_loop(0, far, give, 0)
            own_near, peer_near = near_rows(0), near_rows(OWN)
            for i in range(4):
                after[i][:, at] = jnp.where(own_near, results[i, :OWN, at], before[i][:, at])
                after[4][i, :, at] = jnp.where(
                    peer_near, results[i, OWN:, at], before[4][i, :, at]
                )

        @pl.when(jnp.logical_not(here))
        def _():
            for i in range(4):
                after[i][:, at] = before[i][:, at]
                after[4][i, :, at] = before[4][i, :, at]

        return carry

    @pl.when((step < plan[PAIRS]) | (step == 0))
    def _():
        gather_rows(q, k, v, g, peer, rows)
        lax.fori_loop(0, 2, one, 0)


def head_specs(heads, at):
    steps, width = MINE // heads, heads * HD
    own = [pl.BlockSpec((OWN, width), lambda i, plan: (0, plan[CORE] * steps + at(i, plan)))] * 4
    half = pl.BlockSpec((4, OWN, width), lambda i, plan: (0, 0, at(i, plan)))
    return own, half


def head_scratch(heads):
    return [pltpu.VMEM((4, HALF, heads * HD), jnp.bfloat16)] * 2


PARAMS = pltpu.CompilerParams(vmem_limit_bytes=40 * 1024 * 1024)
HALF_SHAPE = jax.ShapeDtypeStruct((4, OWN, COLS), jnp.bfloat16)
OUT_SHAPES = [jax.ShapeDtypeStruct((OWN, HEADS * HD), jnp.bfloat16)] * 4


def near_call(plan, arrays, peer):
    own, half = head_specs(NEAR_HEADS, lambda i, plan: i)
    return pl.pallas_call(
        near_kernel,
        grid_spec=pltpu.PrefetchScalarGridSpec(
            num_scalar_prefetch=1,
            grid=(MINE // NEAR_HEADS,),
            in_specs=own + [half],
            out_specs=own + [half],
            scratch_shapes=head_scratch(NEAR_HEADS) + [pltpu.VMEM((HD, HALF), jnp.float32)] * 2,
        ),
        out_shape=OUT_SHAPES + [HALF_SHAPE],
        compiler_params=PARAMS,
        name="near_clips",
    )(plan, *arrays, peer)


def cross_call(plan, arrays, peer, arrived, results):
    own, half = head_specs(
        2, lambda i, plan: plan[PAIR] + jnp.minimum(i, jnp.maximum(plan[PAIRS], 1) - 1)
    )
    whole = pl.BlockSpec(arrived.shape, lambda i, plan: (0, 0, 0, 0))
    return pl.pallas_call(
        cross_kernel,
        grid_spec=pltpu.PrefetchScalarGridSpec(
            num_scalar_prefetch=1,
            grid=(MINE // 2,),
            in_specs=own + [half, whole] + own + [half],
            out_specs=own + [half, whole],
            scratch_shapes=head_scratch(2),
        ),
        out_shape=OUT_SHAPES + [HALF_SHAPE, jax.ShapeDtypeStruct(arrived.shape, jnp.bfloat16)],
        input_output_aliases={7 + i: i for i in range(5)},
        compiler_params=PARAMS,
        name="cross_clip",
    )(plan, *arrays, peer, arrived, *results)


def near_slots(plan, body):
    near = plan[NEAR]

    def one_head(head, carry):
        def one(frame, carry):
            row = pl.multiple_of(plan[NEARROW] + FPT * frame, FPT)
            body(head * near + frame, plan[AWAY] + head, row)
            return carry

        return lax.fori_loop(0, near, one, carry)

    lax.fori_loop(0, plan[GONE], one_head, 0)


SLOTS_SHAPE = jax.ShapeDtypeStruct((SLOTS[0], 4, FPT, HD), jnp.bfloat16)


def first_kernel(place, tables, q, k, v, g, plan, mine, give):
    fill_plan(plan, place, tables)
    mine[...] = jnp.zeros_like(mine)
    give[...] = jnp.zeros_like(give)

    def body(slot, head, row):
        @pl.when((row >= OWN) == (plan[CORE] == 1))
        def _():
            at = pl.ds(pl.multiple_of(row & (OWN - 1), FPT), FPT)
            for out, core in ((mine, plan[CORE]), (give, 1 - plan[CORE])):
                col = pl.ds(pl.multiple_of((core * MINE + head) * HD, HD), HD)
                for i, x in enumerate((q, k, v, g)):
                    out[slot, i] = x[at, col]

    near_slots(plan, body)


def first_call(place, tables, arrays):
    return pl.pallas_call(
        first_kernel,
        in_specs=[SMEM] * 2 + [VMEM] * 4,
        out_specs=[SMEM, VMEM, VMEM],
        out_shape=[jax.ShapeDtypeStruct((BRANCH_IN + 1,), jnp.int32), SLOTS_SHAPE, SLOTS_SHAPE],
        compiler_params=PARAMS,
        name="first_blocks",
    )(place, tables, *arrays)


def split_kernel(place, q, k, v, g, out, sems):
    col = pl.ds(pl.multiple_of((1 - (place[1] & 1)) * COLS, COLS), COLS)
    copies = [
        pltpu.make_async_copy(x.at[:, col], out.at[i], sems.at[i])
        for i, x in enumerate((q, k, v, g))
    ]
    for c in copies:
        c.start()
    for c in copies:
        c.wait()


def split_call(place, arrays):
    return pl.pallas_call(
        split_kernel,
        in_specs=[SMEM] + [ANY] * 4,
        out_specs=VMEM,
        out_shape=HALF_SHAPE,
        scratch_shapes=[pltpu.SemaphoreType.DMA((4,))],
        compiler_params=PARAMS,
        name="split_heads",
    )(place, *arrays)


def join_kernel(plan, other, *rest):
    for i, out in enumerate(rest[4:]):
        out[...] = other[i]


def join_call(plan, other, outs):
    width = COLS // JOIN_STEPS
    block = pl.BlockSpec((OWN, width), lambda i, plan: (0, (1 - plan[CORE]) * JOIN_STEPS + i))
    return pl.pallas_call(
        join_kernel,
        grid_spec=pltpu.PrefetchScalarGridSpec(
            num_scalar_prefetch=1,
            grid=(JOIN_STEPS,),
            in_specs=[pl.BlockSpec((4, OWN, width), lambda i, plan: (0, 0, i))] + [ANY] * 4,
            out_specs=[block] * 4,
        ),
        out_shape=OUT_SHAPES,
        input_output_aliases={2 + i: i for i in range(4)},
        compiler_params=PARAMS,
        name="join_halves",
    )(plan, other, *outs)


def unpack_kernel(own, plan, back, *rest):
    outs, sems = rest[4:8], rest[8]
    core = plan[CORE] if own else 1 - plan[CORE]

    def each(act):
        def body(slot, head, row):
            @pl.when((row >= OWN) == (plan[CORE] == 1))
            def _():
                at = pl.ds(pl.multiple_of(row & (OWN - 1), FPT), FPT)
                col = pl.ds(pl.multiple_of((core * MINE + head) * HD, HD), HD)
                for i, out in enumerate(outs):
                    act(
                        pltpu.make_async_copy(back.at[slot, i], out.at[at, col], sems.at[slot, i])
                    )

        near_slots(plan, body)

    each(lambda c: c.start())
    each(lambda c: c.wait())


def unpack_call(plan, back, outs, own):
    return pl.pallas_call(
        functools.partial(unpack_kernel, own),
        in_specs=[SMEM, VMEM] + [ANY] * 4,
        out_specs=[ANY] * 4,
        out_shape=OUT_SHAPES,
        input_output_aliases={2: 0, 3: 1, 4: 2, 5: 3},
        scratch_shapes=[pltpu.SemaphoreType.DMA((back.shape[0], 4))],
        compiler_params=PARAMS,
        name="unpack_own" if own else "unpack_other",
    )(plan, back, *outs)


OTHER_CORE = [(i, i ^ 1) for i in range(4)]
OTHER_CHIP = [(i, i ^ 2) for i in range(4)]


def branch_in(slots, late=False):
    def run(plan, arrays, peer, mine, got):
        if not slots:
            return near_call(plan, arrays, peer), jnp.zeros(SLOTS_SHAPE.shape, jnp.bfloat16)
        leaving = mine[:slots] + got[:slots]
        if late:
            results = near_call(plan, arrays, peer)
            leaving, results = lax.optimization_barrier((leaving, results))
        arrived = lax.ppermute(leaving, "ulysses", OTHER_CHIP)
        if not late:
            results = near_call(plan, arrays, peer)
            results, arrived = lax.optimization_barrier((results, arrived))
        return results, pad_slots(arrived)

    return run


def branch_out(slots):
    def run(plan, results, leaving):
        if slots:
            returned = lax.ppermute(leaving[:slots], "ulysses", OTHER_CHIP)
        other = lax.ppermute(results[4], "ulysses", OTHER_CORE)
        outs = join_call(plan, other, results[:4])
        if not slots:
            return outs, jnp.zeros(SLOTS_SHAPE.shape, jnp.bfloat16)
        outs, returned = lax.optimization_barrier((outs, returned))
        return outs, pad_slots(returned)

    return run


def pad_slots(blocks):
    return jnp.pad(blocks, ((0, SLOTS[0] - blocks.shape[0]), (0, 0), (0, 0), (0, 0)))


def shards(queries, key_rows, values, out_grad, frames, offsets):
    place = jnp.stack([lax.axis_index("dp"), lax.axis_index("ulysses")]).astype(jnp.int32)
    arrays = (queries, key_rows, values, out_grad)
    sent = split_call(place, arrays)
    peer = lax.ppermute(sent, "ulysses", OTHER_CORE)
    tables = jnp.concatenate([frames.T, offsets.T])
    sent, tables, place = lax.optimization_barrier((sent, tables, place))
    plan, mine, give = first_call(place, tables, arrays)
    got = lax.ppermute(give, "ulysses", OTHER_CORE)
    ways_in = [branch_in(n) for n in SLOTS] + [branch_in(n, late=True) for n in LATE_SLOTS]
    results, arrived = lax.switch(plan[BRANCH_IN], ways_in, plan, arrays, peer, mine, got)
    *results, leaving = cross_call(plan, arrays, peer, arrived, results)
    outs, returned = lax.switch(
        plan[BRANCH], [branch_out(n) for n in SLOTS], plan, results, leaving
    )
    returned_other = lax.ppermute(returned, "ulysses", OTHER_CORE)
    outs = unpack_call(plan, returned, outs, own=True)
    outs, returned_other = lax.optimization_barrier((outs, returned_other))
    return tuple(unpack_call(plan, returned_other, outs, own=False))


def solution(mesh):
    rows = P(("dp", "ulysses"), None)
    return jax.shard_map(
        shards,
        mesh=mesh,
        in_specs=(rows, rows, rows, rows, P(), P()),
        out_specs=(rows, rows, rows, rows),
        check_vma=False,
    )
```

```python
import functools
import math

import jax
import jax.numpy as jnp
from jax import lax
from jax.experimental import pallas as pl
from jax.experimental.pallas import tpu as pltpu
from jax.sharding import PartitionSpec as P

HEADS = 20
HD = 128
FPT = 64
FPT_BITS = 6
HALF = 512
OWN = 256
MINE = 10
COLS = MINE * HD
NEG_FILL = -1e30
ANY = pl.BlockSpec(memory_space=pl.ANY)
SMEM = pl.BlockSpec(memory_space=pltpu.SMEM)
VMEM = pl.BlockSpec(memory_space=pltpu.VMEM)
SCALE = 1.0 / math.sqrt(HD)
LOG2E = math.log2(math.e)
ROWS_STEP = 256
JOIN_STEPS = 5
NEAR_HEADS = 2

SLOTS = (20, 18, 15, 12, 10, 0)
LATE_SLOTS = (20, 18, 15, 10)


CORE, B0, E0, B1, E1, PA, PB, FIRST, COUNT, NEAR, FAR, NEARROW, FARROW, AWAY, GONE, PAIR, PAIRS, BRANCH, BRANCH_IN = range(19)


def split_heads(a, b):
    best, heads = jnp.maximum(a, b * (MINE - 1)), 1
    for h in range(2, MINE):
        cost = jnp.maximum(a * h, b * (MINE - h))
        heads = jnp.where(cost < best, h, heads)
        best = jnp.minimum(cost, best)
    return heads, jnp.where((a > 0) & (b > 0), best, 0)


def crossing(tables, group):
    a = b = 0
    for i in range(2):
        begin = tables[2 + i, group]
        end = begin + tables[i, group] * FPT
        crosses = (begin < HALF) & (end > HALF)
        a = jnp.where(crosses, (HALF - begin) >> FPT_BITS, a)
        b = jnp.where(crosses, (end - HALF) >> FPT_BITS, b)
    return (a, b, *split_heads(a, b))


def place_in(choices, cost):
    found = 0
    for i, n in enumerate(choices[1:]):
        found = jnp.where(cost <= n, i + 1, found)
    return found


def fill_plan(plan, place, tables):
    group, core, high = place[0], place[1] & 1, place[1] >> 1
    base = high * HALF
    for i, (begin_at, end_at) in enumerate(((B0, E0), (B1, E1))):
        begin = tables[2 + i, group]
        end = begin + tables[i, group] * FPT
        crosses = (begin < HALF) & (end > HALF)
        plan[begin_at] = jnp.where(crosses, 0, begin - base)
        plan[end_at] = jnp.where(crosses, 0, end - base)
    a, b, h, cost = crossing(tables, group)
    other = crossing(tables, group ^ 2)[3]
    late = (cost > 0) & ((other > cost) | ((other == cost) & ((group & 2) == 2)))
    branch = place_in(SLOTS, cost)
    plan[BRANCH_IN] = jnp.where(late, len(SLOTS) + place_in(LATE_SLOTS, cost), branch)
    second = high == 1
    plan[CORE] = core
    plan[PA] = FPT * a
    plan[PB] = FPT * b
    plan[FIRST] = jnp.where(second, 0, h)
    plan[COUNT] = jnp.where(cost == 0, 0, jnp.where(second, h, MINE - h))
    plan[GONE] = jnp.where(cost == 0, 0, jnp.where(second, MINE - h, h))
    plan[NEAR] = jnp.where(second, b, a)
    plan[FAR] = jnp.where(second, a, b)
    plan[NEARROW] = jnp.where(second, 0, HALF - FPT * a)
    plan[FARROW] = jnp.where(second, HALF - FPT * a, 0)
    plan[PAIR] = jnp.where(second, 0, h >> 1)
    plan[PAIRS] = jnp.where(cost == 0, 0, jnp.where(second, (h + 1) >> 1, MINE // 2 - (h >> 1)))
    plan[AWAY] = jnp.where(second, h, 0)
    plan[BRANCH] = branch


def local_row(plan, position):
    return (position + OWN * plan[CORE]) & (HALF - 1)


def near_clips(plan, position):
    row = local_row(plan, position)
    first = (row >= plan[B0]) & (row < plan[E0])
    second = (row >= plan[B1]) & (row < plan[E1])
    return jnp.where(first, 0, jnp.where(second, 1, -1))


def cross_clip(plan, position):
    row = local_row(plan, position)
    return jnp.where((row < plan[PB]) | (row >= HALF - plan[PA]), 0, -1)


def dot(x, y, dims):
    return lax.dot_general(x, y, (dims, ((), ())), preferred_element_type=jnp.float32)


def attend(label_of, rows, results, head):
    at = pl.ds(pl.multiple_of(head * HD, HD), HD)
    columns = label_of(lax.broadcasted_iota(jnp.int32, (1, HALF), 1))
    k, v = rows[1, :, at], rows[2, :, at]
    blocks = [pl.ds(start, ROWS_STEP) for start in range(0, HALF, ROWS_STEP)]
    labels = [
        label_of(block.start + lax.broadcasted_iota(jnp.int32, (ROWS_STEP, 1), 0))
        for block in blocks
    ]
    q = [rows[0, block, at] for block in blocks]
    g = [rows[3, block, at] for block in blocks]
    scores = [dot(x, k, ((1,), (1,))) for x in q]
    masked = [jnp.where(x == columns, s, NEG_FILL) for x, s in zip(labels, scores)]
    row_max = [jnp.max(s, axis=1, keepdims=True) for s in masked]
    e = [jnp.exp2((s - m) * (SCALE * LOG2E)) for s, m in zip(masked, row_max)]
    row_total = [jnp.sum(x, axis=1, keepdims=True) for x in e]
    inverse = [jnp.where(x >= 0, 1.0 / t, 0.0) for x, t in zip(labels, row_total)]
    probs = [x * i for x, i in zip(e, inverse)]
    probs_low = [x.astype(jnp.bfloat16) for x in probs]
    attended = [dot(x, v, ((1,), (0,))) for x in probs_low]
    dprobs = [dot(x, v, ((1,), (1,))) for x in g]
    dot_term = [
        jnp.sum(x.astype(jnp.float32) * y, axis=1, keepdims=True) for x, y in zip(g, attended)
    ]
    scaled = [x * (i * SCALE) for x, i in zip(e, inverse)]
    dscore = [(x * (d - t)).astype(jnp.bfloat16) for x, d, t in zip(scaled, dprobs, dot_term)]
    query_grad = [dot(x, k, ((1,), (0,))) for x in dscore]
    for block, x, y in zip(blocks, attended, query_grad):
        results[0, block, at] = x.astype(jnp.bfloat16)
        results[1, block, at] = y.astype(jnp.bfloat16)
    key_grad = sum(dot(x, y, ((0,), (0,))) for x, y in zip(q, dscore))
    value_grad = sum(dot(x, y, ((0,), (0,))) for x, y in zip(g, probs_low))
    results[2, :, at] = key_grad.astype(jnp.bfloat16).T
    results[3, :, at] = value_grad.astype(jnp.bfloat16).T


def attend_in_loop(label_of, rows, results, key_total, value_total, head):
    at = pl.ds(pl.multiple_of(head * HD, HD), HD)
    columns = label_of(lax.broadcasted_iota(jnp.int32, (1, HALF), 1))
    k, v = rows[1, :, at], rows[2, :, at]
    key_total[...] = jnp.zeros_like(key_total)
    value_total[...] = jnp.zeros_like(value_total)

    def one(step, carry):
        start = pl.multiple_of(step * ROWS_STEP, ROWS_STEP)
        block = pl.ds(start, ROWS_STEP)
        labels = label_of(start + lax.broadcasted_iota(jnp.int32, (ROWS_STEP, 1), 0))
        q, g = rows[0, block, at], rows[3, block, at]
        masked = jnp.where(labels == columns, dot(q, k, ((1,), (1,))), NEG_FILL)
        row_max = jnp.max(masked, axis=1, keepdims=True)
        e = jnp.exp2((masked - row_max) * (SCALE * LOG2E))
        row_total = jnp.sum(e, axis=1, keepdims=True)
        inverse = jnp.where(labels >= 0, 1.0 / row_total, 0.0)
        probs = e * inverse
        probs_low = probs.astype(jnp.bfloat16)
        attended = dot(probs_low, v, ((1,), (0,)))
        dprobs = dot(g, v, ((1,), (1,)))
        dot_term = jnp.sum(g.astype(jnp.float32) * attended, axis=1, keepdims=True)
        dscore = (e * (inverse * SCALE) * (dprobs - dot_term)).astype(jnp.bfloat16)
        results[0, block, at] = attended.astype(jnp.bfloat16)
        results[1, block, at] = dot(dscore, k, ((1,), (0,))).astype(jnp.bfloat16)
        key_total[...] += dot(q, dscore, ((0,), (0,)))
        value_total[...] += dot(g, probs_low, ((0,), (0,)))
        return carry

    lax.fori_loop(0, HALF // ROWS_STEP, one, 0)
    results[2, :, at] = key_total[...].astype(jnp.bfloat16).T
    results[3, :, at] = value_total[...].astype(jnp.bfloat16).T


def gather_rows(q, k, v, g, peer, rows):
    for i, mine in enumerate((q, k, v, g)):
        rows[i, :OWN, :] = mine[...]
    rows[:, OWN:, :] = peer[...]


def near_kernel(plan, q, k, v, g, peer, out_0, out_1, out_2, out_3, peer_out, *scratch):
    rows, results, key_total, value_total = scratch
    gather_rows(q, k, v, g, peer, rows)

    def one(head, carry):
        labels = functools.partial(near_clips, plan)
        attend_in_loop(labels, rows, results, key_total, value_total, head)
        return carry

    lax.fori_loop(0, NEAR_HEADS, one, 0)
    for i, out in enumerate((out_0, out_1, out_2, out_3)):
        out[...] = results[i, :OWN, :]
    peer_out[...] = results[:, OWN:, :]


def cross_kernel(plan, q, k, v, g, peer, arrived, *rest):
    before, after, (leaving, rows, results) = rest[:5], rest[5:10], rest[10:]
    step = pl.program_id(0)
    far = plan[FAR]
    labels = functools.partial(cross_clip, plan)

    def place(frame):
        return pl.ds(pl.multiple_of(local_row(plan, plan[FARROW] + FPT * frame), FPT), FPT)

    def near_rows(start):
        row = local_row(plan, start + lax.broadcasted_iota(jnp.int32, (OWN, HD), 0))
        return (row >= plan[NEARROW]) & (row < plan[NEARROW] + FPT * plan[NEAR])

    def one(head, carry):
        at = pl.ds(pl.multiple_of(head * HD, HD), HD)
        order = (plan[PAIR] + step) * 2 + head - plan[FIRST]
        here = (order >= 0) & (order < plan[COUNT])

        def take(frame, carry):
            rows[:, place(frame), at] = arrived[order * far + frame]
            return carry

        def give(frame, carry):
            leaving[order * far + frame] = results[:, place(frame), at]
            return carry

        @pl.when(here)
        def _():
            lax.fori_loop(0, far, take, 0)
            attend(labels, rows, results, head)
            lax.fori_loop(0, far, give, 0)
            own_near, peer_near = near_rows(0), near_rows(OWN)
            for i in range(4):
                after[i][:, at] = jnp.where(own_near, results[i, :OWN, at], before[i][:, at])
                after[4][i, :, at] = jnp.where(
                    peer_near, results[i, OWN:, at], before[4][i, :, at]
                )

        @pl.when(jnp.logical_not(here))
        def _():
            for i in range(4):
                after[i][:, at] = before[i][:, at]
                after[4][i, :, at] = before[4][i, :, at]

        return carry

    @pl.when((step < plan[PAIRS]) | (step == 0))
    def _():
        gather_rows(q, k, v, g, peer, rows)
        lax.fori_loop(0, 2, one, 0)


def head_specs(heads, at):
    steps, width = MINE // heads, heads * HD
    own = [pl.BlockSpec((OWN, width), lambda i, plan: (0, plan[CORE] * steps + at(i, plan)))] * 4
    half = pl.BlockSpec((4, OWN, width), lambda i, plan: (0, 0, at(i, plan)))
    return own, half


def head_scratch(heads):
    return [pltpu.VMEM((4, HALF, heads * HD), jnp.bfloat16)] * 2


PARAMS = pltpu.CompilerParams(vmem_limit_bytes=40 * 1024 * 1024)
HALF_SHAPE = jax.ShapeDtypeStruct((4, OWN, COLS), jnp.bfloat16)
OUT_SHAPES = [jax.ShapeDtypeStruct((OWN, HEADS * HD), jnp.bfloat16)] * 4


def near_call(plan, arrays, peer):
    own, half = head_specs(NEAR_HEADS, lambda i, plan: i)
    return pl.pallas_call(
        near_kernel,
        grid_spec=pltpu.PrefetchScalarGridSpec(
            num_scalar_prefetch=1,
            grid=(MINE // NEAR_HEADS,),
            in_specs=own + [half],
            out_specs=own + [half],
            scratch_shapes=head_scratch(NEAR_HEADS) + [pltpu.VMEM((HD, HALF), jnp.float32)] * 2,
        ),
        out_shape=OUT_SHAPES + [HALF_SHAPE],
        compiler_params=PARAMS,
        name="near_clips",
    )(plan, *arrays, peer)


def cross_call(plan, arrays, peer, arrived, results):
    own, half = head_specs(
        2, lambda i, plan: plan[PAIR] + jnp.minimum(i, jnp.maximum(plan[PAIRS], 1) - 1)
    )
    whole = pl.BlockSpec(arrived.shape, lambda i, plan: (0, 0, 0, 0))
    return pl.pallas_call(
        cross_kernel,
        grid_spec=pltpu.PrefetchScalarGridSpec(
            num_scalar_prefetch=1,
            grid=(MINE // 2,),
            in_specs=own + [half, whole] + own + [half],
            out_specs=own + [half, whole],
            scratch_shapes=head_scratch(2),
        ),
        out_shape=OUT_SHAPES + [HALF_SHAPE, jax.ShapeDtypeStruct(arrived.shape, jnp.bfloat16)],
        input_output_aliases={7 + i: i for i in range(5)},
        compiler_params=PARAMS,
        name="cross_clip",
    )(plan, *arrays, peer, arrived, *results)


def near_slots(plan, body):
    near = plan[NEAR]

    def one_head(head, carry):
        def one(frame, carry):
            row = pl.multiple_of(plan[NEARROW] + FPT * frame, FPT)
            body(head * near + frame, plan[AWAY] + head, row)
            return carry

        return lax.fori_loop(0, near, one, carry)

    lax.fori_loop(0, plan[GONE], one_head, 0)


SLOTS_SHAPE = jax.ShapeDtypeStruct((SLOTS[0], 4, FPT, HD), jnp.bfloat16)


def first_kernel(place, tables, q, k, v, g, plan, mine, give):
    fill_plan(plan, place, tables)
    mine[...] = jnp.zeros_like(mine)
    give[...] = jnp.zeros_like(give)

    def body(slot, head, row):
        @pl.when((row >= OWN) == (plan[CORE] == 1))
        def _():
            at = pl.ds(pl.multiple_of(row & (OWN - 1), FPT), FPT)
            for out, core in ((mine, plan[CORE]), (give, 1 - plan[CORE])):
                col = pl.ds(pl.multiple_of((core * MINE + head) * HD, HD), HD)
                for i, x in enumerate((q, k, v, g)):
                    out[slot, i] = x[at, col]

    near_slots(plan, body)


def first_call(place, tables, arrays):
    return pl.pallas_call(
        first_kernel,
        in_specs=[SMEM] * 2 + [VMEM] * 4,
        out_specs=[SMEM, VMEM, VMEM],
        out_shape=[jax.ShapeDtypeStruct((BRANCH_IN + 1,), jnp.int32), SLOTS_SHAPE, SLOTS_SHAPE],
        compiler_params=PARAMS,
        name="first_blocks",
    )(place, tables, *arrays)


def split_kernel(place, q, k, v, g, out, sems):
    col = pl.ds(pl.multiple_of((1 - (place[1] & 1)) * COLS, COLS), COLS)
    copies = [
        pltpu.make_async_copy(x.at[:, col], out.at[i], sems.at[i])
        for i, x in enumerate((q, k, v, g))
    ]
    for c in copies:
        c.start()
    for c in copies:
        c.wait()


def split_call(place, arrays):
    return pl.pallas_call(
        split_kernel,
        in_specs=[SMEM] + [ANY] * 4,
        out_specs=VMEM,
        out_shape=HALF_SHAPE,
        scratch_shapes=[pltpu.SemaphoreType.DMA((4,))],
        compiler_params=PARAMS,
        name="split_heads",
    )(place, *arrays)


def join_kernel(plan, other, *rest):
    for i, out in enumerate(rest[4:]):
        out[...] = other[i]


def join_call(plan, other, outs):
    width = COLS // JOIN_STEPS
    block = pl.BlockSpec((OWN, width), lambda i, plan: (0, (1 - plan[CORE]) * JOIN_STEPS + i))
    return pl.pallas_call(
        join_kernel,
        grid_spec=pltpu.PrefetchScalarGridSpec(
            num_scalar_prefetch=1,
            grid=(JOIN_STEPS,),
            in_specs=[pl.BlockSpec((4, OWN, width), lambda i, plan: (0, 0, i))] + [ANY] * 4,
            out_specs=[block] * 4,
        ),
        out_shape=OUT_SHAPES,
        input_output_aliases={2 + i: i for i in range(4)},
        compiler_params=PARAMS,
        name="join_halves",
    )(plan, other, *outs)


def unpack_kernel(plan, mine, other, *rest):
    outs, sems = rest[4:8], rest[8]

    def each(act):
        def body(slot, head, row):
            @pl.when((row >= OWN) == (plan[CORE] == 1))
            def _():
                at = pl.ds(pl.multiple_of(row & (OWN - 1), FPT), FPT)
                for j, back in enumerate((mine, other)):
                    core = plan[CORE] if j == 0 else 1 - plan[CORE]
                    col = pl.ds(pl.multiple_of((core * MINE + head) * HD, HD), HD)
                    for i, out in enumerate(outs):
                        act(
                            pltpu.make_async_copy(
                                back.at[slot, i], out.at[at, col], sems.at[slot, j, i]
                            )
                        )

        near_slots(plan, body)

    each(lambda c: c.start())
    each(lambda c: c.wait())


def unpack_call(plan, mine, other, outs):
    return pl.pallas_call(
        unpack_kernel,
        in_specs=[SMEM, VMEM, VMEM] + [ANY] * 4,
        out_specs=[ANY] * 4,
        out_shape=OUT_SHAPES,
        input_output_aliases={3: 0, 4: 1, 5: 2, 6: 3},
        scratch_shapes=[pltpu.SemaphoreType.DMA((mine.shape[0], 2, 4))],
        compiler_params=PARAMS,
        name="unpack_cross",
    )(plan, mine, other, *outs)


OTHER_CORE = [(i, i ^ 1) for i in range(4)]
OTHER_CHIP = [(i, i ^ 2) for i in range(4)]


def branch_in(slots, late=False):
    def run(plan, arrays, peer, mine, got):
        if not slots:
            return near_call(plan, arrays, peer), jnp.zeros(SLOTS_SHAPE.shape, jnp.bfloat16)
        leaving = mine[:slots] + got[:slots]
        if late:
            results = near_call(plan, arrays, peer)
            leaving, results = lax.optimization_barrier((leaving, results))
        arrived = lax.ppermute(leaving, "ulysses", OTHER_CHIP)
        if not late:
            results = near_call(plan, arrays, peer)
            results, arrived = lax.optimization_barrier((results, arrived))
        return results, pad_slots(arrived)

    return run


def branch_out(slots):
    def run(plan, results, leaving):
        if slots:
            returned = lax.ppermute(leaving[:slots], "ulysses", OTHER_CHIP)
        other = lax.ppermute(results[4], "ulysses", OTHER_CORE)
        outs = join_call(plan, other, results[:4])
        if not slots:
            return outs, jnp.zeros(SLOTS_SHAPE.shape, jnp.bfloat16)
        outs, returned = lax.optimization_barrier((outs, returned))
        return outs, pad_slots(returned)

    return run


def pad_slots(blocks):
    return jnp.pad(blocks, ((0, SLOTS[0] - blocks.shape[0]), (0, 0), (0, 0), (0, 0)))


def shards(queries, key_rows, values, out_grad, frames, offsets):
    place = jnp.stack([lax.axis_index("dp"), lax.axis_index("ulysses")]).astype(jnp.int32)
    arrays = (queries, key_rows, values, out_grad)
    sent = split_call(place, arrays)
    peer = lax.ppermute(sent, "ulysses", OTHER_CORE)
    tables = jnp.concatenate([frames.T, offsets.T])
    sent, tables, place = lax.optimization_barrier((sent, tables, place))
    plan, mine, give = first_call(place, tables, arrays)
    got = lax.ppermute(give, "ulysses", OTHER_CORE)
    ways_in = [branch_in(n) for n in SLOTS] + [branch_in(n, late=True) for n in LATE_SLOTS]
    results, arrived = lax.switch(plan[BRANCH_IN], ways_in, plan, arrays, peer, mine, got)
    *results, leaving = cross_call(plan, arrays, peer, arrived, results)
    outs, returned = lax.switch(
        plan[BRANCH], [branch_out(n) for n in SLOTS], plan, results, leaving
    )
    returned_other = lax.ppermute(returned, "ulysses", OTHER_CORE)
    return tuple(unpack_call(plan, returned, returned_other, outs))


def solution(mesh):
    rows = P(("dp", "ulysses"), None)
    return jax.shard_map(
        shards,
        mesh=mesh,
        in_specs=(rows, rows, rows, rows, P(), P()),
        out_specs=(rows, rows, rows, rows),
        check_vma=False,
    )
```
